128 devices in a mesh: row: 8 (over y, core), col: 16 (over x, z).
Axes of the slice: x: 4, y: 4, z: 4, core: 2. Of those that a mesh axis runs over, the one named last changes fastest.
Arguments:
- covariance: float32 [4, 4096, 2, 8192], P(None, 'row', None, 'col'), may hold values from 0 to 2, as said below
- band_mask: int32 [32, 32], replicated, may hold values from 0 to 1, as said below
Outputs:
- schur: float32 [4, 4096, 2, 8192], P(None, 'row', None, 'col')
- panels: float32 [4, 4096, 1024], P(None, 'row')
The draws below stay inside these ranges and needn't reach their ends.
Inputs may be any that keep to these rules, and one draw needn't show every extreme that they name: band_mask is symmetric, holds 0 or 1, and is 1 wherever the two tile indices differ by at most 1 and wherever either tile index is below 2. covariance is symmetric, with 1 added on its diagonal; A is positive definite.
All inputs are finite; a program needn't handle non-finite values.
Results may differ from the reference program's by a relative error of at most 0.0003.
Values sent between devices are 32-bit elements; how exact they have to be, the bound alone decides.
A program may use at most 128 MiB of HBM per device.

```python
import jax
import jax.numpy as jnp
from jax import lax

TILE = 512
FEAT = 4
COL_TILES = 2
TILES = 32
ROW_TILES = 4
ORDER = 16384
N_ROW = 8
N_COL = 16


ROOT_THREE = 1.7320508075688772


RANGE_MATERN = 0.2


RANGE_TAPER = 0.35


def draw_band_mask(key, part):
    draws_int = jax.random.randint(key, (TILES, TILES), 0, 8)
    lower_part = jnp.tril((draws_int < 1).astype(jnp.int32))
    symmetric = jnp.maximum(lower_part, lower_part.T)
    places = jnp.arange(TILES, dtype=jnp.int32)
    nearby = (jnp.abs(places[:, None] - places[None, :]) <= 1).astype(jnp.int32)
    leading = jnp.maximum((places[:, None] < 2).astype(jnp.int32), (places[None, :] < 2).astype(jnp.int32))
    return jnp.maximum(jnp.maximum(symmetric, nearby), leading).astype(jnp.int32)


def draw_covariance(key, part):
    points = jax.random.uniform(jax.random.fold_in(key, 11), (FEAT, ORDER), jnp.float32, 0.0, 0.25)
    places = jnp.arange(ORDER, dtype=jnp.int32)

    def one_row(index):
        row_points = lax.dynamic_slice_in_dim(points, index * TILE, TILE, 1)
        squares = jnp.zeros((TILE, ORDER), jnp.float32)
        for feature in range(FEAT):
            offset = row_points[feature][:, None] - points[feature][None, :]
            squares = squares + offset * offset
        distance = jnp.sqrt(squares)
        scaled = ROOT_THREE / RANGE_MATERN * distance
        ratio = distance / RANGE_TAPER
        taper = jnp.maximum(1.0 - ratio, 0.0) ** 4 * (4.0 * ratio + 1.0)
        row_place = lax.dynamic_slice_in_dim(places, index * TILE, TILE, 0)
        same_place = (row_place[:, None] == places[None, :]).astype(jnp.float32)
        return (1.0 + scaled) * jnp.exp(-scaled) * taper + same_place
    full = lax.map(one_row, jnp.arange(TILES, dtype=jnp.int32))
    return full.reshape(ROW_TILES, N_ROW * TILE, COL_TILES, N_COL * TILE)


def setup_inputs(seed: int = 0) -> dict:
    splits = jax.random.split(jax.random.key(seed), 3)
    return {
        "covariance": draw_covariance(jax.random.fold_in(splits[2], 71), 0),
        "band_mask": draw_band_mask(jax.random.fold_in(splits[2], 71), 0),
    }


def solve_below(factor, column, tile_ids, index):
    count = column.shape[0]
    rhs_block = jnp.transpose(column, (2, 0, 1)).reshape(TILE, count * TILE)
    solved = lax.linalg.triangular_solve(factor, rhs_block, left_side=True, lower=True)
    solved = jnp.transpose(solved.reshape(TILE, count, TILE), (1, 2, 0))
    chosen = tile_ids[:, None, None]
    return jnp.where(chosen > index, solved, jnp.where(chosen == index, factor[None], jnp.zeros_like(solved)))

def factor_panels(tall, tile_ids):
    count = tile_ids.shape[0]
    blocks = tall.reshape(count, TILE, 2, TILE)
    first_factor = jnp.linalg.cholesky(blocks[0, :, 0, :])
    panel_zero = solve_below(first_factor, blocks[:, :, 0, :], tile_ids, 0)
    second = blocks[:, :, 1, :] - jnp.einsum('mab,cb->mac', panel_zero, panel_zero[1], precision=lax.Precision.HIGHEST)
    second_factor = jnp.linalg.cholesky(second[1])
    panel_one = solve_below(second_factor, second, tile_ids, 1)
    return (panel_zero, panel_one)

def reference(covariance, band_mask):
    full = covariance.reshape(TILES, TILE, TILES, TILE)
    keep_all = band_mask.astype(jnp.float32)
    tile_ids = jnp.arange(TILES, dtype=jnp.int32)
    tall = (full[:, :, :2, :] * keep_all[:, None, :2, None]).reshape(ORDER, 2 * TILE)
    panel_zero, panel_one = factor_panels(tall, tile_ids)
    flat_zero = panel_zero.reshape(ORDER, TILE)
    flat_one = panel_one.reshape(ORDER, TILE)
    col_keep = (tile_ids >= 2).astype(jnp.float32)

    def one_row(index):
        block = lax.dynamic_index_in_dim(full, index, 0, keepdims=False)
        keep_row = lax.dynamic_index_in_dim(keep_all, index, 0, keepdims=False)
        block = (block * keep_row[None, :, None]).reshape(TILE, ORDER)
        zero_rows = lax.dynamic_slice_in_dim(flat_zero, index * TILE, TILE, 0)
        one_rows = lax.dynamic_slice_in_dim(flat_one, index * TILE, TILE, 0)
        block = block - jnp.dot(zero_rows, flat_zero.T, precision=lax.Precision.HIGHEST)
        block = block - jnp.dot(one_rows, flat_one.T, precision=lax.Precision.HIGHEST)
        row_keep = (index >= 2).astype(jnp.float32)
        block = block.reshape(TILE, TILES, TILE) * (row_keep * col_keep)[None, :, None]
        return block.reshape(TILE, ORDER)
    schur = lax.map(one_row, tile_ids)
    panels = jnp.concatenate([panel_zero, panel_one], axis=2)
    return (schur.reshape(ROW_TILES, N_ROW * TILE, COL_TILES, N_COL * TILE), panels.reshape(ROW_TILES, N_ROW * TILE, 2 * TILE))
```

```python
import functools

import jax
import jax.numpy as jnp
from jax import lax
from jax.experimental import pallas as pl
from jax.experimental.pallas import tpu as pltpu
from jax.sharding import PartitionSpec as P

TILE = 512
B = 128
NB = TILE // B
F32 = jnp.float32
BF16 = jnp.bfloat16
MESH = pl.DeviceIdType.MESH
HIGH = lax.Precision.HIGHEST

TREE_PARENT = {
    4: (0, 0), 7: (4, 3), 8: (4, 0), 5: (4, 1), 11: (7, 0), 6: (7, 3), 1: (5, 2), 3: (7, 2),
    9: (8, 1), 12: (8, 0), 10: (9, 1), 2: (6, 2), 13: (9, 0), 15: (11, 0), 14: (10, 0),
}
TREE_DEPTH = {0: 0, 4: 1, 7: 2, 8: 2, 5: 2, 11: 3, 6: 3, 1: 3, 3: 3, 9: 3, 12: 3, 10: 4, 2: 4, 13: 4, 15: 4, 14: 5}
MAX_DEPTH = 5
CHUNKS = 16
CROWS = TILE // CHUNKS
TCHUNKS = 8
TROWS = TILE // TCHUNKS
WROWS = B // 4


def factor_block(rows):
    n = len(rows)
    x = list(rows)
    sub = lax.broadcasted_iota(jnp.int32, (8, B), 0)
    lane = lax.broadcasted_iota(jnp.int32, (8, B), 1)
    for s in range(n):
        g0 = x[s]
        inside = (lane >= 8 * s) & (lane < 8 * s + 8)
        cols = [jnp.broadcast_to(g0[:, 8 * s + j : 8 * s + j + 1], (8, B)) for j in range(8)]
        a = [[jnp.broadcast_to(cols[j][i : i + 1, :], (8, B)) if i >= j else None for j in range(8)] for i in range(8)]
        gz = jnp.where(inside, (lane - 8 * s == sub).astype(F32), g0)
        g = [jnp.broadcast_to(gz[i : i + 1, :], (8, B)) for i in range(8)]
        l = [[None] * 8 for _ in range(8)]
        r = [None] * 8
        u = [None] * 8
        for j in range(8):
            r[j] = lax.rsqrt(a[j][j])
            u[j] = g[j] * r[j]
            for i in range(j + 1, 8):
                l[i][j] = a[i][j] * r[j]
            for i in range(j + 1, 8):
                for m in range(j + 1, i + 1):
                    a[i][m] = a[i][m] - l[i][j] * l[m][j]
                g[i] = g[i] - l[i][j] * u[j]
        out = u[0]
        for j in range(1, 8):
            out = jnp.where(sub == j, u[j], out)
        for t in range(s + 1, n):
            c = [jnp.broadcast_to(x[t][:, 8 * s + j : 8 * s + j + 1], (8, B)) for j in range(8)]
            acc = jnp.where(inside, 0.0, x[t])
            for j in range(8):
                cj = c[j] * r[j]
                acc = acc - cj * u[j]
                for m in range(j + 1, 8):
                    c[m] = c[m] - l[m][j] * cj
            x[t] = acc
        x[s] = out
    return jnp.concatenate(x, axis=0)


def dot_nn(a, b):
    return jnp.dot(a, b, precision=HIGH, preferred_element_type=F32)


def dot_nt(a, b):
    return lax.dot_general(a, b, (((1,), (1,)), ((), ())), precision=HIGH, preferred_element_type=F32)


def factor_tile(m, w, base, publish):
    rr = lax.broadcasted_iota(jnp.int32, (B, B), 0)
    cc = lax.broadcasted_iota(jnp.int32, (B, B), 1)
    cw = lax.broadcasted_iota(jnp.int32, (B, TILE), 1)

    def step(k, _):
        o = pl.multiple_of(k * B, B)
        rows = [m[pl.ds(pl.multiple_of(o + 8 * s, 8), 8), pl.ds(o, B)] for s in range(B // 8)]
        inv = jnp.where(cc <= rr, factor_block(rows), 0.0)
        inside = (cw >= o) & (cw < o + B)
        row = dot_nn(inv, m[pl.ds(o, B), :])
        row = jnp.where(inside, jnp.concatenate([inv] * NB, axis=1), row)
        m[pl.ds(o, B), :] = row
        w[pl.ds(pl.multiple_of(base + o, B), B), :] = jnp.where(cw < o + B, row, 0.0)
        publish(k)

        def update(i, _):
            oi = pl.multiple_of(i * B, B)
            left = dot_nt(m[pl.ds(oi, B), pl.ds(o, B)], inv)
            old = jnp.where(inside, 0.0, m[pl.ds(oi, B), :])
            m[pl.ds(oi, B), :] = old - dot_nn(left, m[pl.ds(o, B), :])
            return 0

        lax.fori_loop(k + 1, NB, update, 0)
        return 0

    lax.fori_loop(0, NB, step, 0)


def any_of(value, options):
    hit = value == options[0]
    for option in options[1:]:
        hit = hit | (value == option)
    return hit


def exchange_kernel(
    x0, x1, cbuf, tbuf, wout, m, amat, w, csend, crecv, tsend, trecv, wsend, wrecv, asend, arecv, lsem
):
    r = lax.axis_index("row")
    c = lax.axis_index("col")
    y, core = r // 2, r % 2
    x, z = c // 4, c % 4
    sibling = (r + 1 - 2 * core, c)
    around = [
        (r, ((x + 1) % 4) * 4 + z),
        (r, x * 4 + (z + 1) % 4),
        (r, ((x + 3) % 4) * 4 + z),
        (r, x * 4 + (z + 3) % 4),
    ]
    y_next = ((r + 2) % 8, c)
    y_prev = ((r + 6) % 8, c)
    root = (r == 0) & (c == 0)
    proxy = (r == 1) & (c == 0)
    near_root = (r == 0) & any_of(c, (1, 3, 4, 12))
    has_a11 = (r == 1) & (c == 1)

    bar = pltpu.get_barrier_semaphore()
    for dev in around + [y_next, y_prev, sibling]:
        pl.semaphore_signal(bar, inc=1, device_id=dev, device_id_type=MESH)

    @pl.when(near_root)
    def _():
        pl.semaphore_signal(bar, inc=1, device_id=(1, 0), device_id_type=MESH)

    @pl.when(proxy)
    def _():
        for col in (1, 3, 4, 12):
            pl.semaphore_signal(bar, inc=1, device_id=(0, col), device_id_type=MESH)

    @pl.when(has_a11)
    def _():
        pl.semaphore_signal(bar, inc=1, device_id=(0, 0), device_id_type=MESH)

    @pl.when(root)
    def _():
        pl.semaphore_signal(bar, inc=1, device_id=(1, 1), device_id_type=MESH)

    extra = near_root.astype(jnp.int32) + 4 * proxy.astype(jnp.int32) + has_a11.astype(jnp.int32) + root.astype(jnp.int32)
    pl.semaphore_wait(bar, 7 + extra)

    a10 = pltpu.make_async_remote_copy(
        x0.at[0], amat.at[0], asend.at[0], arecv.at[0], device_id=(0, 0), device_id_type=MESH
    )
    a11 = pltpu.make_async_remote_copy(
        x0.at[0], amat.at[1], asend.at[1], arecv.at[1], device_id=(0, 0), device_id_type=MESH
    )

    @pl.when(proxy)
    def _():
        a10.start()

    @pl.when(has_a11)
    def _():
        a11.start()

    first = pltpu.make_async_copy(x0.at[0], m, lsem.at[0])

    @pl.when(root)
    def _():
        first.start()

    place = []
    for s in range(2):
        zr = (z + 4 - s) % 4
        nx, nz = (4 - x) % 4, (4 - zr) % 4
        for q in range(4):
            a, b = ((x, zr), (zr, nx), (nx, nz), (nz, x))[q]
            node = 4 * a + b
            depth = jnp.int32(0)
            for k, v in TREE_DEPTH.items():
                depth = jnp.where(node == k, v, depth)
            flags = []
            for d in range(4):
                senders = [p for p, pd in TREE_PARENT.values() if pd == d]
                flags.append(any_of(node, sorted(senders)) if senders else None)
            place.append((node, depth, flags))

    def crow(chunk):
        return pl.ds(pl.multiple_of(chunk * CROWS, CROWS), CROWS)

    def csend_to(src, slot, dst_slot, d, target, chunk):
        return pltpu.make_async_remote_copy(
            src.at[crow(chunk)],
            cbuf.at[dst_slot, crow(chunk)],
            csend.at[slot, d],
            crecv.at[dst_slot, chunk],
            device_id=target,
            device_id_type=MESH,
        )

    def to_proxy(s, d, q):
        col = around[(d + q) % 4][1]
        return (r == 0) & (col == 0) if s == 1 else None

    def forward(src, s, q, slot, dst_slot, row, chunk, redirect):
        node, depth, flags = place[4 * s + q]
        for d in range(4):
            if flags[d] is None:
                continue
            col = around[(d + q) % 4][1]
            if redirect:
                away = (col == 0) & (r == 0)
                row_d = jnp.where(away, 1, row)
                slot_d = jnp.where(away, 8 + q, dst_slot)
            else:
                row_d, slot_d = row, dst_slot

            @pl.when(flags[d])
            def _():
                csend_to(src, slot, slot_d, d, (row_d, col), chunk).start()

    source = [c == 0, c == 1]

    def send_all(s):
        def go(chunk, _):
            for q in range(4):
                forward(x0.at[q], s, q, 4 * s + q, 4 * s + q, r, chunk, s == 1)
            return 0

        lax.fori_loop(0, CHUNKS, go, 0)

    def trow(chunk):
        return pl.ds(pl.multiple_of(chunk * TROWS, TROWS), TROWS)

    t_on = [y < 3, y != 1]
    t_dev = [y_next, y_prev]
    t_depth = [y, (4 - y) % 4]
    t_source = y == 0

    def t_forward(src, t, chunk):
        @pl.when(t_on[t])
        def _():
            pltpu.make_async_remote_copy(
                src.at[trow(chunk)], tbuf.at[core, t, trow(chunk)], tsend.at[t, 0], trecv.at[core, t, chunk],
                device_id=t_dev[t], device_id_type=MESH,
            ).start()

        pltpu.make_async_remote_copy(
            src.at[trow(chunk)], tbuf.at[core, t, trow(chunk)], tsend.at[t, 1], trecv.at[core, t, chunk],
            device_id=sibling, device_id_type=MESH,
        ).start()

    t_src = [x0.at[0], x1]

    @pl.when(t_source)
    def _():
        def go(chunk, _):
            for t in range(2):
                t_forward(t_src[t], t, chunk)
            return 0

        lax.fori_loop(0, TCHUNKS, go, 0)
        for t in range(2):
            pltpu.make_async_copy(t_src[t], tbuf.at[core, t], lsem.at[1 + t]).start()

    for s in range(2):

        @pl.when(source[s])
        def _():
            send_all(s)
            for q in range(4):
                pltpu.make_async_copy(x0.at[q], cbuf.at[4 * s + q], lsem.at[3 + q]).start()

    w_on = []
    for q in range(4):
        _, _, flags = place[q]
        on = [(flags[d] & (y == 0), around[(d + q) % 4]) if flags[d] is not None else None for d in range(4)]
        if q % 2 == 0:
            on.append((y < 3, y_next))
        else:
            on.append((y != 1, y_prev))
        on.append((core == 0, sibling))
        w_on.append(on)

    def w_rows(block, q):
        return pl.ds(pl.multiple_of(block * B + q * WROWS, WROWS), WROWS)

    def w_forward(block, q):
        for d, entry in enumerate(w_on[q]):
            if entry is None:
                continue
            flag, dev = entry

            @pl.when(flag & (core == 0))
            def _():
                pltpu.make_async_remote_copy(
                    w.at[w_rows(block, q)], w.at[w_rows(block, q)], wsend.at[q, d], wrecv.at[block, q],
                    device_id=dev, device_id_type=MESH,
                ).start()

    def w_wait(block, q):
        pltpu.make_async_copy(w.at[w_rows(block, q)], w.at[w_rows(block, q)], wrecv.at[block, q]).wait()

    def w_pass(mat):
        def go(k, _):
            for q in range(4):
                w_wait(mat * NB + k, q)
                w_forward(mat * NB + k, q)
            return 0

        lax.fori_loop(0, NB, go, 0)

    def c_wait(slot, chunk):
        pltpu.make_async_copy(cbuf.at[slot, crow(chunk)], cbuf.at[slot, crow(chunk)], crecv.at[slot, chunk]).wait()

    def t_wait(k, t, chunk):
        pltpu.make_async_copy(tbuf.at[k, t, trow(chunk)], tbuf.at[k, t, trow(chunk)], trecv.at[k, t, chunk]).wait()

    @pl.when(root)
    def _():
        first.wait()

        def publish(base):
            def go(k):
                for q in range(4):
                    w_forward(base + k, q)

            return go

        factor_tile(m, w, 0, publish(0))
        a10.wait_recv()
        left = dot_nt(amat[0], w[0:TILE, :])
        w[TILE : 2 * TILE, :] = left
        for k in range(NB):
            publish(NB)(k)
        a11.wait_recv()
        m[...] = amat[1] - dot_nt(left, left)
        factor_tile(m, w, 2 * TILE, publish(2 * NB))
        for q in range(4):

            def drain(chunk, _):
                c_wait(4 + q, chunk)
                return 0

            lax.fori_loop(0, CHUNKS, drain, 0)

    @pl.when(jnp.logical_not(root))
    def _():
        def go(k, _):
            for t in range(2):
                chunk = k - t_depth[t]

                @pl.when((chunk >= 0) & (chunk < TCHUNKS) & (y != 0))
                def _():
                    t_wait(core, t, chunk)
                    t_forward(tbuf.at[core, t], t, chunk)

            for s in range(2):
                for q in range(4):
                    _, depth, _ = place[4 * s + q]
                    chunk = k - depth

                    @pl.when((chunk >= 0) & (chunk < CHUNKS) & jnp.logical_not(source[s]))
                    def _():
                        c_wait(4 * s + q, chunk)
                        forward(cbuf.at[4 * s + q], s, q, 4 * s + q, 4 * s + q, r, chunk, s == 1)

                    if s == 1:

                        @pl.when((chunk >= 0) & (chunk < CHUNKS) & proxy)
                        def _():
                            c_wait(8 + q, chunk)
                            csend_to(cbuf.at[8 + q], 8 + q, 4 + q, 4, (0, 0), chunk).start()
                            forward(cbuf.at[8 + q], s, q, 8 + q, 4 + q, 0, chunk, False)

            @pl.when(k == CHUNKS - 1)
            def _():
                w_pass(0)

            @pl.when(k == CHUNKS + 1)
            def _():
                w_pass(1)

            return 0

        lax.fori_loop(0, CHUNKS + MAX_DEPTH, go, 0)
        w_pass(2)

    for t in range(2):

        def drain_t(chunk, _):
            t_wait(1 - core, t, chunk)
            return 0

        lax.fori_loop(0, TCHUNKS, drain_t, 0)

    out = pltpu.make_async_copy(w, wout, lsem.at[7])
    out.start()

    for slot in range(12):
        s = 0 if slot < 4 else 1
        q = slot % 4
        _, _, flags = place[4 * s + q]
        for d in range(5):
            flag = jnp.bool_(True) if d == 4 else flags[d]
            if flag is None or (d == 4 and slot < 8):
                continue
            if slot >= 8:
                flag = flag & proxy
            elif s == 1:
                flag = flag & jnp.logical_not(root)

            @pl.when(flag)
            def _():
                pltpu.make_async_copy(cbuf.at[slot], cbuf.at[slot], csend.at[slot, d]).wait()

    for t in range(2):

        @pl.when(t_on[t])
        def _():
            pltpu.make_async_copy(tbuf.at[0, t], tbuf.at[0, t], tsend.at[t, 0]).wait()

        pltpu.make_async_copy(tbuf.at[0, t], tbuf.at[0, t], tsend.at[t, 1]).wait()

    for q in range(4):
        for d, entry in enumerate(w_on[q]):
            if entry is None:
                continue

            @pl.when(entry[0] & (core == 0))
            def _():
                rows = 3 * NB * WROWS
                pltpu.make_async_copy(w.at[0:rows], w.at[0:rows], wsend.at[q, d]).wait()

    @pl.when(t_source)
    def _():
        for t in range(2):
            pltpu.make_async_copy(t_src[t], tbuf.at[core, t], lsem.at[1 + t]).wait()

    for s in range(2):

        @pl.when(source[s])
        def _():
            for q in range(4):
                pltpu.make_async_copy(x0.at[q], cbuf.at[4 * s + q], lsem.at[3 + q]).wait()

    @pl.when(proxy)
    def _():
        a10.wait_send()

    @pl.when(has_a11)
    def _():
        a11.wait_send()

    out.wait()


def exchange(x0, x1):
    any_space = pl.BlockSpec(memory_space=pl.ANY)
    dma = pltpu.SemaphoreType.DMA
    return pl.pallas_call(
        exchange_kernel,
        out_shape=(
            jax.ShapeDtypeStruct((12, TILE, TILE), F32),
            jax.ShapeDtypeStruct((2, 2, TILE, TILE), F32),
            jax.ShapeDtypeStruct((3 * TILE, TILE), F32),
        ),
        in_specs=[any_space, any_space],
        out_specs=(any_space, any_space, any_space),
        scratch_shapes=[
            pltpu.VMEM((TILE, TILE), F32),
            pltpu.VMEM((2, TILE, TILE), F32),
            pltpu.VMEM((3 * TILE, TILE), F32),
            dma((12, 5)),
            dma((12, CHUNKS)),
            dma((2, 2)),
            dma((2, 2, TCHUNKS)),
            dma((4, 6)),
            dma((3 * NB, 4)),
            dma((2,)),
            dma((2,)),
            dma((8,)),
        ],
        compiler_params=pltpu.CompilerParams(
            collective_id=0, has_side_effects=True, vmem_limit_bytes=48 * 2**20
        ),
        name="exchange",
    )(x0, x1)


def split(a):
    hi = a.astype(BF16)
    return hi, (a - hi.astype(F32)).astype(BF16)


def mm(a, b):
    return jnp.dot(a, b, preferred_element_type=F32)


def mm_t(a, b):
    return lax.dot_general(a, b, (((1,), (1,)), ((), ())), preferred_element_type=F32)


def product(a, b, dot):
    return dot(a[0], b[0]) + (dot(a[0], b[1]) + dot(a[1], b[0]))


def finish_kernel(keep, cov, c0, c1, tb, wo, schur, panel, wh, wl, pth, ptl, ph, plo):
    q = pl.program_id(0)
    r = lax.axis_index("row")
    c = lax.axis_index("col")
    i_tile = q * 8 + r

    @pl.when(q == 0)
    def _():
        hi, lo = split(wo[...])
        wh[...] = hi
        wl[...] = lo
        w00 = (wh[0:TILE], wl[0:TILE])
        l10 = (wh[TILE : 2 * TILE], wl[TILE : 2 * TILE])
        w11 = (wh[2 * TILE :], wl[2 * TILE :])
        for t in range(2):
            cols = slice(t * TILE, (t + 1) * TILE)
            p0 = split(product(w00, split(tb[0, t]), mm))
            pth[0:TILE, cols] = p0[0]
            ptl[0:TILE, cols] = p0[1]
            rest = tb[1, t] - product(l10, p0, mm)
            p1 = split(product(w11, split(rest), mm))
            pth[TILE:, cols] = p1[0]
            ptl[TILE:, cols] = p1[1]

    w00 = (wh[0:TILE], wl[0:TILE])
    l10 = (wh[TILE : 2 * TILE], wl[TILE : 2 * TILE])
    w11 = (wh[2 * TILE :], wl[2 * TILE :])
    rr = lax.broadcasted_iota(jnp.int32, (TILE, TILE), 0)
    cc = lax.broadcasted_iota(jnp.int32, (TILE, TILE), 1)
    p0 = product(split(c0[0]), w00, mm_t)
    p0 = jnp.where((i_tile != 0) | (rr >= cc), p0, 0.0)
    panel[0, :, 0:TILE] = p0
    p0s = split(p0)
    ph[:, 0:TILE] = p0s[0]
    plo[:, 0:TILE] = p0s[1]
    rest = c1[0] - product(p0s, l10, mm_t)
    p1 = product(split(rest), w11, mm_t)
    p1 = jnp.where((i_tile > 1) | ((i_tile == 1) & (rr >= cc)), p1, 0.0)
    panel[0, :, TILE:] = p1
    p1s = split(p1)
    ph[:, TILE:] = p1s[0]
    plo[:, TILE:] = p1s[1]

    for n in range(4):
        t = n // 2
        j_tile = t * 16 + c
        alive = ((i_tile >= 2) & (j_tile >= 2)).astype(F32)
        mask = keep[i_tile, j_tile].astype(F32) * alive
        cols = slice(n * 256, (n + 1) * 256)
        acc = product((ph[...], plo[...]), (pth[:, cols], ptl[:, cols]), mm)
        for h in range(2):
            k = 2 * ((n % 2) * 2 + h) + t
            a = cov[0, :, k, :]
            schur[0, :, k, :] = a * mask - acc[:, h * 128 : (h + 1) * 128] * alive


def finish(keep, cov, cbuf, tbuf, w):
    return pl.pallas_call(
        finish_kernel,
        grid=(4,),
        out_shape=(
            jax.ShapeDtypeStruct((4, TILE, 8, 128), F32),
            jax.ShapeDtypeStruct((4, TILE, 2 * TILE), F32),
        ),
        in_specs=[
            pl.BlockSpec(memory_space=pltpu.SMEM),
            pl.BlockSpec((1, TILE, 8, 128), lambda q: (q, 0, 0, 0)),
            pl.BlockSpec((1, TILE, TILE), lambda q: (q, 0, 0)),
            pl.BlockSpec((1, TILE, TILE), lambda q: (q + 4, 0, 0)),
            pl.BlockSpec(memory_space=pltpu.VMEM),
            pl.BlockSpec(memory_space=pltpu.VMEM),
        ],
        out_specs=(
            pl.BlockSpec((1, TILE, 8, 128), lambda q: (q, 0, 0, 0)),
            pl.BlockSpec((1, TILE, 2 * TILE), lambda q: (q, 0, 0)),
        ),
        scratch_shapes=[
            pltpu.VMEM((3 * TILE, TILE), BF16),
            pltpu.VMEM((3 * TILE, TILE), BF16),
            pltpu.VMEM((2 * TILE, 2 * TILE), BF16),
            pltpu.VMEM((2 * TILE, 2 * TILE), BF16),
            pltpu.VMEM((TILE, 2 * TILE), BF16),
            pltpu.VMEM((TILE, 2 * TILE), BF16),
        ],
        compiler_params=pltpu.CompilerParams(vmem_limit_bytes=56 * 2**20),
        name="finish",
    )(keep, cov, cbuf, cbuf, tbuf, w)


def body(covariance, band_mask):
    x0 = covariance[:, :, 0, :]
    x1 = covariance[0, :, 1, :]
    cbuf, tbuf, w = exchange(x0, x1)
    cov = covariance.reshape(4, TILE, 2, 4, 128).transpose(0, 1, 3, 2, 4).reshape(4, TILE, 8, 128)
    schur, panels = finish(band_mask, cov, cbuf, tbuf, w)
    schur = schur.reshape(4, TILE, 4, 2, 128).transpose(0, 1, 3, 2, 4).reshape(4, TILE, 2, TILE)
    return (schur, panels)


def solution(mesh):
    return jax.shard_map(
        body,
        mesh=mesh,
        in_specs=(P(None, "row", None, "col"), P()),
        out_specs=(P(None, "row", None, "col"), P(None, "row", None)),
        check_vma=False,
    )
```

```python
import functools

import jax
import jax.numpy as jnp
from jax import lax
from jax.experimental import pallas as pl
from jax.experimental.pallas import tpu as pltpu
from jax.sharding import PartitionSpec as P

TILE = 512
B = 128
NB = TILE // B
F32 = jnp.float32
BF16 = jnp.bfloat16
MESH = pl.DeviceIdType.MESH
HIGH = lax.Precision.HIGHEST

TREE_PARENT = {
    4: (0, 0), 7: (4, 3), 8: (4, 0), 5: (4, 1), 11: (7, 0), 6: (7, 3), 1: (5, 2), 3: (7, 2),
    9: (8, 1), 12: (8, 0), 10: (9, 1), 2: (6, 2), 13: (9, 0), 15: (11, 0), 14: (10, 0),
}
TREE_DEPTH = {0: 0, 4: 1, 7: 2, 8: 2, 5: 2, 11: 3, 6: 3, 1: 3, 3: 3, 9: 3, 12: 3, 10: 4, 2: 4, 13: 4, 15: 4, 14: 5}
MAX_DEPTH = 5
CHUNKS = 8
CROWS = TILE // CHUNKS
TCHUNKS = 4
TROWS = TILE // TCHUNKS
TRI = NB * (NB + 1) // 2
FIRST = (0, TRI, TRI + NB * NB)
PIECES = 2 * TRI + NB * NB


def factor_block(rows):
    n = len(rows)
    x = list(rows)
    sub = lax.broadcasted_iota(jnp.int32, (8, B), 0)
    lane = lax.broadcasted_iota(jnp.int32, (8, B), 1)
    for s in range(n):
        g0 = x[s]
        inside = (lane >= 8 * s) & (lane < 8 * s + 8)
        cols = [jnp.broadcast_to(g0[:, 8 * s + j : 8 * s + j + 1], (8, B)) for j in range(8)]
        a = [[jnp.broadcast_to(cols[j][i : i + 1, :], (8, B)) if i >= j else None for j in range(8)] for i in range(8)]
        gz = jnp.where(inside, (lane - 8 * s == sub).astype(F32), g0)
        g = [jnp.broadcast_to(gz[i : i + 1, :], (8, B)) for i in range(8)]
        l = [[None] * 8 for _ in range(8)]
        r = [None] * 8
        u = [None] * 8
        for j in range(8):
            r[j] = lax.rsqrt(a[j][j])
            u[j] = g[j] * r[j]
            for i in range(j + 1, 8):
                l[i][j] = a[i][j] * r[j]
            for i in range(j + 1, 8):
                for m in range(j + 1, i + 1):
                    a[i][m] = a[i][m] - l[i][j] * l[m][j]
                g[i] = g[i] - l[i][j] * u[j]
        out = u[0]
        for j in range(1, 8):
            out = jnp.where(sub == j, u[j], out)
        for t in range(s + 1, n):
            c = [jnp.broadcast_to(x[t][:, 8 * s + j : 8 * s + j + 1], (8, B)) for j in range(8)]
            acc = jnp.where(inside, 0.0, x[t])
            for j in range(8):
                cj = c[j] * r[j]
                acc = acc - cj * u[j]
                for m in range(j + 1, 8):
                    c[m] = c[m] - l[m][j] * cj
            x[t] = acc
        x[s] = out
    return jnp.concatenate(x, axis=0)


def dot_nn(a, b):
    return jnp.dot(a, b, precision=HIGH, preferred_element_type=F32)


def dot_nt(a, b):
    return lax.dot_general(a, b, (((1,), (1,)), ((), ())), precision=HIGH, preferred_element_type=F32)


def factor_tile(m, w, first, send):
    rr = lax.broadcasted_iota(jnp.int32, (B, B), 0)
    cc = lax.broadcasted_iota(jnp.int32, (B, B), 1)
    cw = lax.broadcasted_iota(jnp.int32, (B, TILE), 1)

    def step(k, _):
        o = pl.multiple_of(k * B, B)
        rows = [m[pl.ds(pl.multiple_of(o + 8 * s, 8), 8), pl.ds(o, B)] for s in range(B // 8)]
        inv = jnp.where(cc <= rr, factor_block(rows), 0.0)
        inside = (cw >= o) & (cw < o + B)
        row = dot_nn(inv, m[pl.ds(o, B), :])
        row = jnp.where(inside, jnp.concatenate([inv] * NB, axis=1), row)
        m[pl.ds(o, B), :] = row

        def publish(n, _):
            piece = first + k * (k + 1) // 2 + n
            w[piece] = m[pl.ds(o, B), pl.ds(pl.multiple_of(n * B, B), B)]
            send(piece)
            return 0

        lax.fori_loop(0, k + 1, publish, 0)

        def update(i, _):
            oi = pl.multiple_of(i * B, B)
            left = dot_nt(m[pl.ds(oi, B), pl.ds(o, B)], inv)
            old = jnp.where(inside, 0.0, m[pl.ds(oi, B), :])
            m[pl.ds(oi, B), :] = old - dot_nn(left, m[pl.ds(o, B), :])
            return 0

        lax.fori_loop(k + 1, NB, update, 0)
        return 0

    lax.fori_loop(0, NB, step, 0)


def any_of(value, options):
    hit = value == options[0]
    for option in options[1:]:
        hit = hit | (value == option)
    return hit


def exchange_kernel(
    x0, x1, cbuf, tbuf, wout, m, amat, w, bounce, csend, crecv, tsend, trecv, wsend, wrecv, asend, arecv, lsem
):
    r = lax.axis_index("row")
    c = lax.axis_index("col")
    y, core = r // 2, r % 2
    x, z = c // 4, c % 4
    sibling = (r + 1 - 2 * core, c)
    around = [
        (r, ((x + 1) % 4) * 4 + z),
        (r, x * 4 + (z + 1) % 4),
        (r, ((x + 3) % 4) * 4 + z),
        (r, x * 4 + (z + 3) % 4),
    ]
    y_next = ((r + 2) % 8, c)
    y_prev = ((r + 6) % 8, c)
    root = (r == 0) & (c == 0)
    proxy = (r == 1) & (c == 0)
    near_root = (r == 0) & any_of(c, (1, 3, 4, 12))
    has_a11 = (r == 1) & (c == 1)

    bar = pltpu.get_barrier_semaphore()
    for dev in around + [y_next, y_prev, sibling]:
        pl.semaphore_signal(bar, inc=1, device_id=dev, device_id_type=MESH)

    @pl.when(near_root)
    def _():
        pl.semaphore_signal(bar, inc=1, device_id=(1, 0), device_id_type=MESH)

    @pl.when(proxy)
    def _():
        for col in (1, 3, 4, 12):
            pl.semaphore_signal(bar, inc=1, device_id=(0, col), device_id_type=MESH)

    @pl.when(has_a11)
    def _():
        pl.semaphore_signal(bar, inc=1, device_id=(0, 0), device_id_type=MESH)

    @pl.when(root)
    def _():
        pl.semaphore_signal(bar, inc=1, device_id=(1, 1), device_id_type=MESH)

    extra = near_root.astype(jnp.int32) + 4 * proxy.astype(jnp.int32) + has_a11.astype(jnp.int32) + root.astype(jnp.int32)
    pl.semaphore_wait(bar, 7 + extra)

    a10 = pltpu.make_async_remote_copy(
        x0.at[0], amat.at[0], asend.at[0], arecv.at[0], device_id=(0, 0), device_id_type=MESH
    )
    a11 = pltpu.make_async_remote_copy(
        x0.at[0], amat.at[1], asend.at[1], arecv.at[1], device_id=(0, 0), device_id_type=MESH
    )

    @pl.when(proxy)
    def _():
        a10.start()

    @pl.when(has_a11)
    def _():
        a11.start()

    first = pltpu.make_async_copy(x0.at[0], m, lsem.at[0])

    @pl.when(root)
    def _():
        first.start()

    place = []
    for s in range(2):
        zr = (z + 4 - s) % 4
        nx, nz = (4 - x) % 4, (4 - zr) % 4
        for q in range(4):
            a, b = ((x, zr), (zr, nx), (nx, nz), (nz, x))[q]
            node = 4 * a + b
            depth = jnp.int32(0)
            for k, v in TREE_DEPTH.items():
                depth = jnp.where(node == k, v, depth)
            flags = []
            for d in range(4):
                senders = [p for p, pd in TREE_PARENT.values() if pd == d]
                flags.append(any_of(node, sorted(senders)) if senders else None)
            place.append((node, depth, flags))

    def crow(chunk):
        return pl.ds(pl.multiple_of(chunk * CROWS, CROWS), CROWS)

    def csend_to(src, slot, dst_slot, d, target, chunk):
        return pltpu.make_async_remote_copy(
            src.at[crow(chunk)],
            cbuf.at[dst_slot, crow(chunk)],
            csend.at[slot, d],
            crecv.at[dst_slot, chunk],
            device_id=target,
            device_id_type=MESH,
        )

    def to_proxy(s, d, q):
        col = around[(d + q) % 4][1]
        return (r == 0) & (col == 0) if s == 1 else None

    def forward(src, s, q, slot, dst_slot, row, chunk, redirect):
        node, depth, flags = place[4 * s + q]
        for d in range(4):
            if flags[d] is None:
                continue
            col = around[(d + q) % 4][1]
            if redirect:
                away = (col == 0) & (r == 0)
                row_d = jnp.where(away, 1, row)
                slot_d = jnp.where(away, 8 + q, dst_slot)
            else:
                row_d, slot_d = row, dst_slot

            @pl.when(flags[d])
            def _():
                csend_to(src, slot, slot_d, d, (row_d, col), chunk).start()

    source = [c == 0, c == 1]

    def send_all(s):
        def go(chunk, _):
            for q in range(4):
                forward(x0.at[q], s, q, 4 * s + q, 4 * s + q, r, chunk, s == 1)
            return 0

        lax.fori_loop(0, CHUNKS, go, 0)

    def trow(chunk):
        return pl.ds(pl.multiple_of(chunk * TROWS, TROWS), TROWS)

    t_on = [y < 3, y != 1]
    t_dev = [y_next, y_prev]
    t_depth = [y, (4 - y) % 4]
    t_source = y == 0

    def t_forward(src, t, chunk):
        @pl.when(t_on[t])
        def _():
            pltpu.make_async_remote_copy(
                src.at[trow(chunk)], tbuf.at[core, t, trow(chunk)], tsend.at[t, 0], trecv.at[core, t, chunk],
                device_id=t_dev[t], device_id_type=MESH,
            ).start()

        pltpu.make_async_remote_copy(
            src.at[trow(chunk)], tbuf.at[core, t, trow(chunk)], tsend.at[t, 1], trecv.at[core, t, chunk],
            device_id=sibling, device_id_type=MESH,
        ).start()

    t_src = [x0.at[0], x1]

    @pl.when(t_source)
    def _():
        def go(chunk, _):
            for t in range(2):
                t_forward(t_src[t], t, chunk)
            return 0

        lax.fori_loop(0, TCHUNKS, go, 0)
        for t in range(2):
            pltpu.make_async_copy(t_src[t], bounce.at[4 + t], lsem.at[1 + t]).start()

    for s in range(2):

        @pl.when(source[s])
        def _():
            send_all(s)
            for q in range(4):
                pltpu.make_async_copy(x0.at[q], bounce.at[q], lsem.at[3 + q]).start()
            for q in range(4):
                pltpu.make_async_copy(x0.at[q], bounce.at[q], lsem.at[3 + q]).wait()
                pltpu.make_async_copy(bounce.at[q], cbuf.at[4 * s + q], lsem.at[3 + q]).start()

    @pl.when(t_source)
    def _():
        for t in range(2):
            pltpu.make_async_copy(t_src[t], bounce.at[4 + t], lsem.at[1 + t]).wait()
            pltpu.make_async_copy(bounce.at[4 + t], tbuf.at[core, t], lsem.at[1 + t]).start()

    w_on = [
        ((y == 0) & (z == 0) & (x < 2), around[0]),
        ((y == 0) & (z == 0) & (x == 0), around[2]),
        ((y == 0) & (z < 2), around[1]),
        ((y == 0) & (z == 0), around[3]),
        (y < 2, y_next),
        (y == 0, y_prev),
        (core == 0, sibling),
    ]

    def w_send(piece):
        for d, (flag, dev) in enumerate(w_on):

            @pl.when(flag & (core == 0))
            def _():
                pltpu.make_async_remote_copy(
                    w.at[piece], w.at[piece], wsend.at[d], wrecv.at[piece], device_id=dev, device_id_type=MESH
                ).start()

    def w_pass(begin, end):
        def go(piece, _):
            pltpu.make_async_copy(w.at[piece], w.at[piece], wrecv.at[piece]).wait()
            w_send(piece)
            return 0

        lax.fori_loop(begin, end, go, 0)

    def c_wait(slot, chunk):
        pltpu.make_async_copy(cbuf.at[slot, crow(chunk)], cbuf.at[slot, crow(chunk)], crecv.at[slot, chunk]).wait()

    def t_wait(k, t, chunk):
        pltpu.make_async_copy(tbuf.at[k, t, trow(chunk)], tbuf.at[k, t, trow(chunk)], trecv.at[k, t, chunk]).wait()

    @pl.when(root)
    def _():
        first.wait()

        factor_tile(m, w, FIRST[0], w_send)
        big_r = lax.broadcasted_iota(jnp.int32, (TILE, TILE), 0)
        big_c = lax.broadcasted_iota(jnp.int32, (TILE, TILE), 1)
        inv00 = jnp.where(big_r // B >= big_c // B, m[...], 0.0)
        a10.wait_recv()
        left = dot_nt(amat[0], inv00)
        amat[0] = left

        def publish(n, _):
            rows, cols = (pl.ds(pl.multiple_of(v * B, B), B) for v in (n // NB, n % NB))
            w[FIRST[1] + n] = amat[0, rows, cols]
            w_send(FIRST[1] + n)
            return 0

        lax.fori_loop(0, NB * NB, publish, 0)
        a11.wait_recv()
        m[...] = amat[1] - dot_nt(left, left)
        factor_tile(m, w, FIRST[2], w_send)
        for q in range(4):

            def drain(chunk, _):
                c_wait(4 + q, chunk)
                return 0

            lax.fori_loop(0, CHUNKS, drain, 0)

    @pl.when(jnp.logical_not(root))
    def _():
        def go(k, _):
            for t in range(2):
                chunk = k - t_depth[t]

                @pl.when((chunk >= 0) & (chunk < TCHUNKS) & (y != 0))
                def _():
                    t_wait(core, t, chunk)
                    t_forward(tbuf.at[core, t], t, chunk)

            for s in range(2):
                for q in range(4):
                    _, depth, _ = place[4 * s + q]
                    chunk = k - depth

                    @pl.when((chunk >= 0) & (chunk < CHUNKS) & jnp.logical_not(source[s]))
                    def _():
                        c_wait(4 * s + q, chunk)
                        forward(cbuf.at[4 * s + q], s, q, 4 * s + q, 4 * s + q, r, chunk, s == 1)

                    if s == 1:

                        @pl.when((chunk >= 0) & (chunk < CHUNKS) & proxy)
                        def _():
                            c_wait(8 + q, chunk)
                            csend_to(cbuf.at[8 + q], 8 + q, 4 + q, 4, (0, 0), chunk).start()
                            forward(cbuf.at[8 + q], s, q, 8 + q, 4 + q, 0, chunk, False)

            @pl.when(k == 5)
            def _():
                w_pass(FIRST[0], FIRST[1])

            @pl.when(k == 7)
            def _():
                w_pass(FIRST[1], FIRST[2])

            return 0

        lax.fori_loop(0, CHUNKS + MAX_DEPTH, go, 0)
        w_pass(FIRST[2], PIECES)

    for t in range(2):

        def drain_t(chunk, _):
            t_wait(1 - core, t, chunk)
            return 0

        lax.fori_loop(0, TCHUNKS, drain_t, 0)

    out = pltpu.make_async_copy(w, wout, lsem.at[7])
    out.start()

    for slot in range(12):
        s = 0 if slot < 4 else 1
        q = slot % 4
        _, _, flags = place[4 * s + q]
        for d in range(5):
            flag = jnp.bool_(True) if d == 4 else flags[d]
            if flag is None or (d == 4 and slot < 8):
                continue
            if slot >= 8:
                flag = flag & proxy
            elif s == 1:
                flag = flag & jnp.logical_not(root)

            @pl.when(flag)
            def _():
                pltpu.make_async_copy(cbuf.at[slot], cbuf.at[slot], csend.at[slot, d]).wait()

    for t in range(2):

        @pl.when(t_on[t])
        def _():
            pltpu.make_async_copy(tbuf.at[0, t], tbuf.at[0, t], tsend.at[t, 0]).wait()

        pltpu.make_async_copy(tbuf.at[0, t], tbuf.at[0, t], tsend.at[t, 1]).wait()

    for d, (flag, _) in enumerate(w_on):

        @pl.when(flag & (core == 0))
        def _():
            pltpu.make_async_copy(w, w, wsend.at[d]).wait()

    @pl.when(t_source)
    def _():
        for t in range(2):
            pltpu.make_async_copy(bounce.at[4 + t], tbuf.at[core, t], lsem.at[1 + t]).wait()

    for s in range(2):

        @pl.when(source[s])
        def _():
            for q in range(4):
                pltpu.make_async_copy(bounce.at[q], cbuf.at[4 * s + q], lsem.at[3 + q]).wait()

    @pl.when(proxy)
    def _():
        a10.wait_send()

    @pl.when(has_a11)
    def _():
        a11.wait_send()

    out.wait()


def exchange(x0, x1):
    any_space = pl.BlockSpec(memory_space=pl.ANY)
    dma = pltpu.SemaphoreType.DMA
    return pl.pallas_call(
        exchange_kernel,
        out_shape=(
            jax.ShapeDtypeStruct((12, TILE, TILE), F32),
            jax.ShapeDtypeStruct((2, 2, TILE, TILE), F32),
            jax.ShapeDtypeStruct((PIECES, B, B), F32),
        ),
        in_specs=[any_space, any_space],
        out_specs=(any_space, any_space, any_space),
        scratch_shapes=[
            pltpu.VMEM((TILE, TILE), F32),
            pltpu.VMEM((2, TILE, TILE), F32),
            pltpu.VMEM((PIECES, B, B), F32),
            pltpu.VMEM((6, TILE, TILE), F32),
            dma((12, 5)),
            dma((12, CHUNKS)),
            dma((2, 2)),
            dma((2, 2, TCHUNKS)),
            dma((7,)),
            dma((PIECES,)),
            dma((2,)),
            dma((2,)),
            dma((8,)),
        ],
        compiler_params=pltpu.CompilerParams(
            collective_id=0, has_side_effects=True, vmem_limit_bytes=48 * 2**20
        ),
        name="exchange",
    )(x0, x1)


def split(a):
    hi = a.astype(BF16)
    return hi, (a - hi.astype(F32)).astype(BF16)


def mm(a, b):
    return jnp.dot(a, b, preferred_element_type=F32)


def mm_t(a, b):
    return lax.dot_general(a, b, (((1,), (1,)), ((), ())), preferred_element_type=F32)


def product(a, b, dot):
    return dot(a[0], b[0]) + (dot(a[0], b[1]) + dot(a[1], b[0]))


def finish_kernel(keep, cov, c0, c1, tb, wo, schur, panel, wh, wl, pth, ptl, ph, plo):
    q = pl.program_id(0)
    r = lax.axis_index("row")
    c = lax.axis_index("col")
    i_tile = q * 8 + r

    @pl.when(q == 0)
    def _():
        for mat in range(3):
            for i in range(NB):
                for j in range(NB):
                    at = (slice(mat * TILE + i * B, mat * TILE + (i + 1) * B), slice(j * B, (j + 1) * B))
                    if mat != 1 and j > i:
                        wh[at] = jnp.zeros((B, B), BF16)
                        wl[at] = jnp.zeros((B, B), BF16)
                    else:
                        piece = FIRST[mat] + (i * NB + j if mat == 1 else i * (i + 1) // 2 + j)
                        wh[at], wl[at] = split(wo[piece])
        w00 = (wh[0:TILE], wl[0:TILE])
        l10 = (wh[TILE : 2 * TILE], wl[TILE : 2 * TILE])
        w11 = (wh[2 * TILE :], wl[2 * TILE :])
        for t in range(2):
            cols = slice(t * TILE, (t + 1) * TILE)
            p0 = split(product(w00, split(tb[0, t]), mm))
            pth[0:TILE, cols] = p0[0]
            ptl[0:TILE, cols] = p0[1]
            rest = tb[1, t] - product(l10, p0, mm)
            p1 = split(product(w11, split(rest), mm))
            pth[TILE:, cols] = p1[0]
            ptl[TILE:, cols] = p1[1]

    w00 = (wh[0:TILE], wl[0:TILE])
    l10 = (wh[TILE : 2 * TILE], wl[TILE : 2 * TILE])
    w11 = (wh[2 * TILE :], wl[2 * TILE :])
    rr = lax.broadcasted_iota(jnp.int32, (TILE, TILE), 0)
    cc = lax.broadcasted_iota(jnp.int32, (TILE, TILE), 1)
    p0 = product(split(c0[0]), w00, mm_t)
    p0 = jnp.where((i_tile != 0) | (rr >= cc), p0, 0.0)
    panel[0, :, 0:TILE] = p0
    p0s = split(p0)
    ph[:, 0:TILE] = p0s[0]
    plo[:, 0:TILE] = p0s[1]
    rest = c1[0] - product(p0s, l10, mm_t)
    p1 = product(split(rest), w11, mm_t)
    p1 = jnp.where((i_tile > 1) | ((i_tile == 1) & (rr >= cc)), p1, 0.0)
    panel[0, :, TILE:] = p1
    p1s = split(p1)
    ph[:, TILE:] = p1s[0]
    plo[:, TILE:] = p1s[1]

    for n in range(4):
        t = n // 2
        j_tile = t * 16 + c
        alive = ((i_tile >= 2) & (j_tile >= 2)).astype(F32)
        mask = keep[i_tile, j_tile].astype(F32) * alive
        cols = slice(n * 256, (n + 1) * 256)
        acc = product((ph[...], plo[...]), (pth[:, cols], ptl[:, cols]), mm)
        for h in range(2):
            k = 2 * ((n % 2) * 2 + h) + t
            a = cov[0, :, k, :]
            schur[0, :, k, :] = a * mask - acc[:, h * 128 : (h + 1) * 128] * alive


def finish(keep, cov, cbuf, tbuf, w):
    return pl.pallas_call(
        finish_kernel,
        grid=(4,),
        out_shape=(
            jax.ShapeDtypeStruct((4, TILE, 8, 128), F32),
            jax.ShapeDtypeStruct((4, TILE, 2 * TILE), F32),
        ),
        in_specs=[
            pl.BlockSpec(memory_space=pltpu.SMEM),
            pl.BlockSpec((1, TILE, 8, 128), lambda q: (q, 0, 0, 0)),
            pl.BlockSpec((1, TILE, TILE), lambda q: (q, 0, 0)),
            pl.BlockSpec((1, TILE, TILE), lambda q: (q + 4, 0, 0)),
            pl.BlockSpec(memory_space=pltpu.VMEM),
            pl.BlockSpec(memory_space=pltpu.VMEM),
        ],
        out_specs=(
            pl.BlockSpec((1, TILE, 8, 128), lambda q: (q, 0, 0, 0)),
            pl.BlockSpec((1, TILE, 2 * TILE), lambda q: (q, 0, 0)),
        ),
        scratch_shapes=[
            pltpu.VMEM((3 * TILE, TILE), BF16),
            pltpu.VMEM((3 * TILE, TILE), BF16),
            pltpu.VMEM((2 * TILE, 2 * TILE), BF16),
            pltpu.VMEM((2 * TILE, 2 * TILE), BF16),
            pltpu.VMEM((TILE, 2 * TILE), BF16),
            pltpu.VMEM((TILE, 2 * TILE), BF16),
        ],
        compiler_params=pltpu.CompilerParams(vmem_limit_bytes=56 * 2**20),
        name="finish",
    )(keep, cov, cbuf, cbuf, tbuf, w)


def body(covariance, band_mask):
    x0 = covariance[:, :, 0, :]
    x1 = covariance[0, :, 1, :]
    cbuf, tbuf, w = exchange(x0, x1)
    cov = covariance.reshape(4, TILE, 2, 4, 128).transpose(0, 1, 3, 2, 4).reshape(4, TILE, 8, 128)
    schur, panels = finish(band_mask, cov, cbuf, tbuf, w)
    schur = schur.reshape(4, TILE, 4, 2, 128).transpose(0, 1, 3, 2, 4).reshape(4, TILE, 2, TILE)
    return (schur, panels)


def solution(mesh):
    return jax.shard_map(
        body,
        mesh=mesh,
        in_specs=(P(None, "row", None, "col"), P()),
        out_specs=(P(None, "row", None, "col"), P(None, "row", None)),
        check_vma=False,
    )
```

```python
import functools

import jax
import jax.numpy as jnp
from jax import lax
from jax.experimental import pallas as pl
from jax.experimental.pallas import tpu as pltpu
from jax.sharding import PartitionSpec as P

TILE = 512
B = 128
NB = TILE // B
F32 = jnp.float32
BF16 = jnp.bfloat16
MESH = pl.DeviceIdType.MESH
HIGH = lax.Precision.HIGHEST

TREE_PARENT = {
    4: (0, 0), 7: (4, 3), 8: (4, 0), 5: (4, 1), 11: (7, 0), 6: (7, 3), 1: (5, 2), 3: (7, 2),
    9: (8, 1), 12: (8, 0), 10: (9, 1), 2: (6, 2), 13: (9, 0), 15: (11, 0), 14: (10, 0),
}
TREE_DEPTH = {0: 0, 4: 1, 7: 2, 8: 2, 5: 2, 11: 3, 6: 3, 1: 3, 3: 3, 9: 3, 12: 3, 10: 4, 2: 4, 13: 4, 15: 4, 14: 5}
MAX_DEPTH = 5
CHUNKS = 8
CROWS = TILE // CHUNKS
TCHUNKS = 4
TROWS = TILE // TCHUNKS
TRI = NB * (NB + 1) // 2
FIRST = (0, TRI, TRI + NB * NB)
PIECES = 2 * TRI + NB * NB


def factor_block(rows):
    n = len(rows)
    x = list(rows)
    sub = lax.broadcasted_iota(jnp.int32, (8, B), 0)
    lane = lax.broadcasted_iota(jnp.int32, (8, B), 1)
    for s in range(n):
        g0 = x[s]
        inside = (lane >= 8 * s) & (lane < 8 * s + 8)
        cols = [jnp.broadcast_to(g0[:, 8 * s + j : 8 * s + j + 1], (8, B)) for j in range(8)]
        a = [[jnp.broadcast_to(cols[j][i : i + 1, :], (8, B)) if i >= j else None for j in range(8)] for i in range(8)]
        gz = jnp.where(inside, (lane - 8 * s == sub).astype(F32), g0)
        g = [jnp.broadcast_to(gz[i : i + 1, :], (8, B)) for i in range(8)]
        l = [[None] * 8 for _ in range(8)]
        r = [None] * 8
        u = [None] * 8
        for j in range(8):
            r[j] = lax.rsqrt(a[j][j])
            u[j] = g[j] * r[j]
            for i in range(j + 1, 8):
                l[i][j] = a[i][j] * r[j]
            for i in range(j + 1, 8):
                for m in range(j + 1, i + 1):
                    a[i][m] = a[i][m] - l[i][j] * l[m][j]
                g[i] = g[i] - l[i][j] * u[j]
        out = u[0]
        for j in range(1, 8):
            out = jnp.where(sub == j, u[j], out)
        for t in range(s + 1, n):
            c = [jnp.broadcast_to(x[t][:, 8 * s + j : 8 * s + j + 1], (8, B)) for j in range(8)]
            acc = jnp.where(inside, 0.0, x[t])
            for j in range(8):
                cj = c[j] * r[j]
                acc = acc - cj * u[j]
                for m in range(j + 1, 8):
                    c[m] = c[m] - l[m][j] * cj
            x[t] = acc
        x[s] = out
    return jnp.concatenate(x, axis=0)


def dot_nn(a, b):
    return jnp.dot(a, b, precision=HIGH, preferred_element_type=F32)


def dot_nt(a, b):
    return lax.dot_general(a, b, (((1,), (1,)), ((), ())), precision=HIGH, preferred_element_type=F32)


def factor_tile(m, w, first, send):
    rr = lax.broadcasted_iota(jnp.int32, (B, B), 0)
    cc = lax.broadcasted_iota(jnp.int32, (B, B), 1)
    cw = lax.broadcasted_iota(jnp.int32, (B, TILE), 1)

    def step(k, _):
        o = pl.multiple_of(k * B, B)
        rows = [m[pl.ds(pl.multiple_of(o + 8 * s, 8), 8), pl.ds(o, B)] for s in range(B // 8)]
        inv = jnp.where(cc <= rr, factor_block(rows), 0.0)
        inside = (cw >= o) & (cw < o + B)
        row = dot_nn(inv, m[pl.ds(o, B), :])
        row = jnp.where(inside, jnp.concatenate([inv] * NB, axis=1), row)
        m[pl.ds(o, B), :] = row

        def publish(n, _):
            piece = first + k * (k + 1) // 2 + n
            w[piece] = m[pl.ds(o, B), pl.ds(pl.multiple_of(n * B, B), B)]
            send(piece)
            return 0

        lax.fori_loop(0, k + 1, publish, 0)

        def update(i, _):
            oi = pl.multiple_of(i * B, B)
            left = dot_nt(m[pl.ds(oi, B), pl.ds(o, B)], inv)
            old = jnp.where(inside, 0.0, m[pl.ds(oi, B), :])
            m[pl.ds(oi, B), :] = old - dot_nn(left, m[pl.ds(o, B), :])
            return 0

        lax.fori_loop(k + 1, NB, update, 0)
        return 0

    lax.fori_loop(0, NB, step, 0)


def any_of(value, options):
    hit = value == options[0]
    for option in options[1:]:
        hit = hit | (value == option)
    return hit


def exchange_kernel(
    x0, x1, cbuf, tbuf, wout, m, amat, w, bounce, csend, crecv, tsend, trecv, wsend, wrecv, asend, arecv, lsem
):
    r = lax.axis_index("row")
    c = lax.axis_index("col")
    y, core = r // 2, r % 2
    x, z = c // 4, c % 4
    sibling = (r + 1 - 2 * core, c)
    around = [
        (r, ((x + 1) % 4) * 4 + z),
        (r, x * 4 + (z + 1) % 4),
        (r, ((x + 3) % 4) * 4 + z),
        (r, x * 4 + (z + 3) % 4),
    ]
    y_next = ((r + 2) % 8, c)
    y_prev = ((r + 6) % 8, c)
    root = (r == 0) & (c == 0)
    proxy = (r == 1) & (c == 0)
    near_root = (r == 0) & any_of(c, (1, 3, 4, 12))
    has_a11 = (r == 1) & (c == 1)

    bar = pltpu.get_barrier_semaphore()
    for dev in around + [y_next, y_prev, sibling]:
        pl.semaphore_signal(bar, inc=1, device_id=dev, device_id_type=MESH)

    @pl.when(near_root)
    def _():
        pl.semaphore_signal(bar, inc=1, device_id=(1, 0), device_id_type=MESH)

    @pl.when(proxy)
    def _():
        for col in (1, 3, 4, 12):
            pl.semaphore_signal(bar, inc=1, device_id=(0, col), device_id_type=MESH)

    @pl.when(has_a11)
    def _():
        pl.semaphore_signal(bar, inc=1, device_id=(0, 0), device_id_type=MESH)

    @pl.when(root)
    def _():
        pl.semaphore_signal(bar, inc=1, device_id=(1, 1), device_id_type=MESH)

    extra = near_root.astype(jnp.int32) + 4 * proxy.astype(jnp.int32) + has_a11.astype(jnp.int32) + root.astype(jnp.int32)
    pl.semaphore_wait(bar, 7 + extra)

    a10 = pltpu.make_async_remote_copy(
        x0.at[0], amat.at[0], asend.at[0], arecv.at[0], device_id=(0, 0), device_id_type=MESH
    )
    a11 = pltpu.make_async_remote_copy(
        x0.at[0], amat.at[1], asend.at[1], arecv.at[1], device_id=(0, 0), device_id_type=MESH
    )

    @pl.when(proxy)
    def _():
        a10.start()

    @pl.when(has_a11)
    def _():
        a11.start()

    first = pltpu.make_async_copy(x0.at[0], m, lsem.at[0])

    @pl.when(root)
    def _():
        first.start()

    place = []
    for s in range(2):
        zr = (z + 4 - s) % 4
        nx, nz = (4 - x) % 4, (4 - zr) % 4
        for q in range(4):
            a, b = ((x, zr), (zr, nx), (nx, nz), (nz, x))[q]
            node = 4 * a + b
            depth = jnp.int32(0)
            for k, v in TREE_DEPTH.items():
                depth = jnp.where(node == k, v, depth)
            flags = []
            for d in range(4):
                senders = [p for p, pd in TREE_PARENT.values() if pd == d]
                flags.append(any_of(node, sorted(senders)) if senders else None)
            place.append((node, depth, flags))

    def crow(chunk):
        return pl.ds(pl.multiple_of(chunk * CROWS, CROWS), CROWS)

    def csend_to(src, slot, dst_slot, d, target, chunk):
        return pltpu.make_async_remote_copy(
            src.at[crow(chunk)],
            cbuf.at[dst_slot, crow(chunk)],
            csend.at[slot, d],
            crecv.at[dst_slot, chunk],
            device_id=target,
            device_id_type=MESH,
        )

    def to_proxy(s, d, q):
        col = around[(d + q) % 4][1]
        return (r == 0) & (col == 0) if s == 1 else None

    def forward(src, s, q, slot, dst_slot, row, chunk, redirect):
        node, depth, flags = place[4 * s + q]
        for d in range(4):
            if flags[d] is None:
                continue
            col = around[(d + q) % 4][1]
            if redirect:
                away = (col == 0) & (r == 0)
                row_d = jnp.where(away, 1, row)
                slot_d = jnp.where(away, 8 + q, dst_slot)
            else:
                row_d, slot_d = row, dst_slot

            @pl.when(flags[d])
            def _():
                csend_to(src, slot, slot_d, d, (row_d, col), chunk).start()

    source = [c == 0, c == 1]

    def send_all(s):
        def go(chunk, _):
            for q in range(4):
                forward(x0.at[q], s, q, 4 * s + q, 4 * s + q, r, chunk, s == 1)
            return 0

        lax.fori_loop(0, CHUNKS, go, 0)

    def trow(chunk):
        return pl.ds(pl.multiple_of(chunk * TROWS, TROWS), TROWS)

    t_on = [y < 3, y != 1]
    t_dev = [y_next, y_prev]
    t_depth = [y, (4 - y) % 4]
    t_source = y == 0

    def t_forward(src, t, chunk):
        @pl.when(t_on[t])
        def _():
            pltpu.make_async_remote_copy(
                src.at[trow(chunk)], tbuf.at[core, t, trow(chunk)], tsend.at[t, 0], trecv.at[core, t, chunk],
                device_id=t_dev[t], device_id_type=MESH,
            ).start()

        pltpu.make_async_remote_copy(
            src.at[trow(chunk)], tbuf.at[core, t, trow(chunk)], tsend.at[t, 1], trecv.at[core, t, chunk],
            device_id=sibling, device_id_type=MESH,
        ).start()

    t_src = [x0.at[0], x1]

    @pl.when(t_source)
    def _():
        @pl.when(root)
        def _():
            def go(chunk, _):
                for t in range(2):
                    t_forward(t_src[t], t, chunk)
                return 0

            lax.fori_loop(0, TCHUNKS, go, 0)

        for t in range(2):
            pltpu.make_async_copy(t_src[t], bounce.at[4 + t], lsem.at[1 + t]).start()

    for s in range(2):

        @pl.when(source[s])
        def _():
            if s == 0:

                @pl.when(root)
                def _():
                    send_all(s)

            for q in range(4):
                pltpu.make_async_copy(x0.at[q], bounce.at[q], lsem.at[3 + q]).start()
            for q in range(4):
                pltpu.make_async_copy(x0.at[q], bounce.at[q], lsem.at[3 + q]).wait()
                pltpu.make_async_copy(bounce.at[q], cbuf.at[4 * s + q], lsem.at[3 + q]).start()

    @pl.when(t_source)
    def _():
        for t in range(2):
            pltpu.make_async_copy(t_src[t], bounce.at[4 + t], lsem.at[1 + t]).wait()
            pltpu.make_async_copy(bounce.at[4 + t], tbuf.at[core, t], lsem.at[1 + t]).start()

    w_on, w_depth = [], []
    for q in range(4):
        _, depth, flags = place[q]
        on = [(flags[d] & (y == 0), around[(d + q) % 4]) if flags[d] is not None else None for d in range(4)]
        on.append((y < 3, y_next) if q % 2 == 0 else (y != 1, y_prev))
        on.append((core == 0, sibling))
        w_on.append(on)
        w_depth.append(depth + t_depth[q % 2])

    def w_send(n, q):
        for d, entry in enumerate(w_on[q]):
            if entry is None:
                continue
            flag, dev = entry

            @pl.when(flag & (core == 0))
            def _():
                pltpu.make_async_remote_copy(
                    w.at[4 * n + q], w.at[4 * n + q], wsend.at[q, d], wrecv.at[4 * n + q],
                    device_id=dev, device_id_type=MESH,
                ).start()

    def w_send_piece(piece):
        for q in range(4):

            @pl.when(piece % 4 == q)
            def _():
                w_send(piece // 4, q)

    def w_wait(piece):
        pltpu.make_async_copy(w.at[piece], w.at[piece], wrecv.at[piece]).wait()

    w_steps = PIECES // 4 + MAX_DEPTH + 3

    def w_pass(begin, end):
        def go(k, _):
            for q in range(4):
                n = k - w_depth[q]

                @pl.when((n >= 0) & (n < PIECES // 4) & (core == 0))
                def _():
                    w_wait(4 * n + q)
                    w_send(n, q)

            return 0

        lax.fori_loop(begin, end, go, 0)

    def w_rest():
        @pl.when(core == 1)
        def _():
            def go(piece, _):
                w_wait(piece)
                return 0

            lax.fori_loop(0, PIECES, go, 0)

    def c_wait(slot, chunk):
        pltpu.make_async_copy(cbuf.at[slot, crow(chunk)], cbuf.at[slot, crow(chunk)], crecv.at[slot, chunk]).wait()

    def t_wait(k, t, chunk):
        pltpu.make_async_copy(tbuf.at[k, t, trow(chunk)], tbuf.at[k, t, trow(chunk)], trecv.at[k, t, chunk]).wait()

    @pl.when(root)
    def _():
        first.wait()

        factor_tile(m, w, FIRST[0], w_send_piece)
        big_r = lax.broadcasted_iota(jnp.int32, (TILE, TILE), 0)
        big_c = lax.broadcasted_iota(jnp.int32, (TILE, TILE), 1)
        inv00 = jnp.where(big_r // B >= big_c // B, m[...], 0.0)
        a10.wait_recv()
        left = dot_nt(amat[0], inv00)
        amat[0] = left

        def publish(n, _):
            rows, cols = (pl.ds(pl.multiple_of(v * B, B), B) for v in (n // NB, n % NB))
            w[FIRST[1] + n] = amat[0, rows, cols]
            w_send_piece(FIRST[1] + n)
            return 0

        lax.fori_loop(0, NB * NB, publish, 0)
        a11.wait_recv()
        m[...] = amat[1] - dot_nt(left, left)
        factor_tile(m, w, FIRST[2], w_send_piece)
        for q in range(4):

            def drain(chunk, _):
                c_wait(4 + q, chunk)
                return 0

            lax.fori_loop(0, CHUNKS, drain, 0)

    @pl.when(jnp.logical_not(root))
    def _():
        def go(k, _):
            for t in range(2):
                chunk = k - t_depth[t]

                @pl.when((chunk >= 0) & (chunk < TCHUNKS) & (y != 0))
                def _():
                    t_wait(core, t, chunk)
                    t_forward(tbuf.at[core, t], t, chunk)

                @pl.when((chunk < TCHUNKS) & (y == 0))
                def _():
                    t_forward(t_src[t], t, chunk)

            for s in range(2):
                for q in range(4):
                    _, depth, _ = place[4 * s + q]
                    chunk = k - depth

                    @pl.when((chunk >= 0) & (chunk < CHUNKS) & jnp.logical_not(source[s]))
                    def _():
                        c_wait(4 * s + q, chunk)
                        forward(cbuf.at[4 * s + q], s, q, 4 * s + q, 4 * s + q, r, chunk, s == 1)

                    @pl.when((chunk < CHUNKS) & source[s])
                    def _():
                        d = 0
                        col = around[q][1]
                        away = (s == 1) & (col == 0) & (r == 0)
                        csend_to(
                            x0.at[q], 4 * s + q, jnp.where(away, 8 + q, 4 * s + q), d, (jnp.where(away, 1, r), col), chunk
                        ).start()

                    if s == 1:

                        @pl.when((chunk >= 0) & (chunk < CHUNKS) & proxy)
                        def _():
                            c_wait(8 + q, chunk)
                            csend_to(cbuf.at[8 + q], 8 + q, 4 + q, 4, (0, 0), chunk).start()
                            forward(cbuf.at[8 + q], s, q, 8 + q, 4 + q, 0, chunk, False)

            @pl.when(k >= 6)
            def _():
                w_pass(2 * (k - 6), 2 * (k - 6) + 2)

            return 0

        lax.fori_loop(0, CHUNKS + MAX_DEPTH, go, 0)
        w_pass(2 * (CHUNKS + MAX_DEPTH - 6), w_steps)
        w_rest()

    for t in range(2):

        def drain_t(chunk, _):
            t_wait(1 - core, t, chunk)
            return 0

        lax.fori_loop(0, TCHUNKS, drain_t, 0)

    out = pltpu.make_async_copy(w, wout, lsem.at[7])
    out.start()

    for slot in range(12):
        s = 0 if slot < 4 else 1
        q = slot % 4
        _, _, flags = place[4 * s + q]
        for d in range(5):
            flag = jnp.bool_(True) if d == 4 else flags[d]
            if flag is None or (d == 4 and slot < 8):
                continue
            if slot >= 8:
                flag = flag & proxy
            elif s == 1:
                flag = flag & jnp.logical_not(root)

            @pl.when(flag)
            def _():
                pltpu.make_async_copy(cbuf.at[slot], cbuf.at[slot], csend.at[slot, d]).wait()

    for t in range(2):

        @pl.when(t_on[t])
        def _():
            pltpu.make_async_copy(tbuf.at[0, t], tbuf.at[0, t], tsend.at[t, 0]).wait()

        pltpu.make_async_copy(tbuf.at[0, t], tbuf.at[0, t], tsend.at[t, 1]).wait()

    for q in range(4):
        for d, entry in enumerate(w_on[q]):
            if entry is None:
                continue

            @pl.when(entry[0] & (core == 0))
            def _():
                pltpu.make_async_copy(w.at[0 : PIECES // 4], w.at[0 : PIECES // 4], wsend.at[q, d]).wait()

    @pl.when(t_source)
    def _():
        for t in range(2):
            pltpu.make_async_copy(bounce.at[4 + t], tbuf.at[core, t], lsem.at[1 + t]).wait()

    for s in range(2):

        @pl.when(source[s])
        def _():
            for q in range(4):
                pltpu.make_async_copy(bounce.at[q], cbuf.at[4 * s + q], lsem.at[3 + q]).wait()

    @pl.when(proxy)
    def _():
        a10.wait_send()

    @pl.when(has_a11)
    def _():
        a11.wait_send()

    out.wait()


def exchange(x0, x1):
    any_space = pl.BlockSpec(memory_space=pl.ANY)
    dma = pltpu.SemaphoreType.DMA
    return pl.pallas_call(
        exchange_kernel,
        out_shape=(
            jax.ShapeDtypeStruct((12, TILE, TILE), F32),
            jax.ShapeDtypeStruct((2, 2, TILE, TILE), F32),
            jax.ShapeDtypeStruct((PIECES, B, B), F32),
        ),
        in_specs=[any_space, any_space],
        out_specs=(any_space, any_space, any_space),
        scratch_shapes=[
            pltpu.VMEM((TILE, TILE), F32),
            pltpu.VMEM((2, TILE, TILE), F32),
            pltpu.VMEM((PIECES, B, B), F32),
            pltpu.VMEM((6, TILE, TILE), F32),
            dma((12, 5)),
            dma((12, CHUNKS)),
            dma((2, 2)),
            dma((2, 2, TCHUNKS)),
            dma((4, 6)),
            dma((PIECES,)),
            dma((2,)),
            dma((2,)),
            dma((8,)),
        ],
        compiler_params=pltpu.CompilerParams(
            collective_id=0, has_side_effects=True, vmem_limit_bytes=60 * 2**20
        ),
        name="exchange",
    )(x0, x1)


def pick_kernel(cov, x0, x1):
    for k in range(NB):
        x0[0, :, k * B : (k + 1) * B] = cov[0, :, 2 * k, :]

    @pl.when(pl.program_id(0) == 0)
    def _():
        for k in range(NB):
            x1[:, k * B : (k + 1) * B] = cov[0, :, 2 * k + 1, :]


def pick(cov):
    return pl.pallas_call(
        pick_kernel,
        grid=(4,),
        out_shape=(jax.ShapeDtypeStruct((4, TILE, TILE), F32), jax.ShapeDtypeStruct((TILE, TILE), F32)),
        in_specs=[pl.BlockSpec((1, TILE, 8, 128), lambda q: (q, 0, 0, 0))],
        out_specs=(
            pl.BlockSpec((1, TILE, TILE), lambda q: (q, 0, 0)),
            pl.BlockSpec((TILE, TILE), lambda q: (0, 0)),
        ),
        compiler_params=pltpu.CompilerParams(vmem_limit_bytes=60 * 2**20),
        name="pick",
    )(cov)


def split(a):
    hi = a.astype(BF16)
    return hi, (a - hi.astype(F32)).astype(BF16)


def mm(a, b):
    return jnp.dot(a, b, preferred_element_type=F32)


def mm_t(a, b):
    return lax.dot_general(a, b, (((1,), (1,)), ((), ())), preferred_element_type=F32)


def product(a, b, dot):
    return dot(a[0], b[0]) + (dot(a[0], b[1]) + dot(a[1], b[0]))


def lower_product(w, b):
    half = TILE // 2
    top = product([v[:half, :half] for v in w], [v[:half] for v in b], mm)
    return jnp.concatenate([top, product([v[half:] for v in w], b, mm)], axis=0)


def product_lower(a, w):
    half = TILE // 2
    left = product([v[:, :half] for v in a], [v[:half, :half] for v in w], mm_t)
    return jnp.concatenate([left, product(a, [v[half:] for v in w], mm_t)], axis=1)


def finish_kernel(keep, cov, c0, c1, tb, wo, schur, panel, wh, wl, pth, ptl, ph, plo):
    q = pl.program_id(0)
    r = lax.axis_index("row")
    c = lax.axis_index("col")
    i_tile = q * 8 + r

    @pl.when(q == 0)
    def _():
        for mat in range(3):
            for i in range(NB):
                for j in range(NB):
                    at = (slice(mat * TILE + i * B, mat * TILE + (i + 1) * B), slice(j * B, (j + 1) * B))
                    if mat != 1 and j > i:
                        wh[at] = jnp.zeros((B, B), BF16)
                        wl[at] = jnp.zeros((B, B), BF16)
                    else:
                        piece = FIRST[mat] + (i * NB + j if mat == 1 else i * (i + 1) // 2 + j)
                        wh[at], wl[at] = split(wo[piece])
        w00 = (wh[0:TILE], wl[0:TILE])
        l10 = (wh[TILE : 2 * TILE], wl[TILE : 2 * TILE])
        w11 = (wh[2 * TILE :], wl[2 * TILE :])
        for t in range(2):
            cols = slice(t * TILE, (t + 1) * TILE)
            p0 = split(lower_product(w00, split(tb[0, t])))
            pth[0:TILE, cols] = p0[0]
            ptl[0:TILE, cols] = p0[1]
            rest = tb[1, t] - product(l10, p0, mm)
            p1 = split(lower_product(w11, split(rest)))
            pth[TILE:, cols] = p1[0]
            ptl[TILE:, cols] = p1[1]

    w00 = (wh[0:TILE], wl[0:TILE])
    l10 = (wh[TILE : 2 * TILE], wl[TILE : 2 * TILE])
    w11 = (wh[2 * TILE :], wl[2 * TILE :])
    rr = lax.broadcasted_iota(jnp.int32, (TILE, TILE), 0)
    cc = lax.broadcasted_iota(jnp.int32, (TILE, TILE), 1)
    p0 = product_lower(split(c0[0]), w00)
    p0 = jnp.where((i_tile != 0) | (rr >= cc), p0, 0.0)
    panel[0, :, 0:TILE] = p0
    p0s = split(p0)
    ph[:, 0:TILE] = p0s[0]
    plo[:, 0:TILE] = p0s[1]
    rest = c1[0] - product(p0s, l10, mm_t)
    p1 = product_lower(split(rest), w11)
    p1 = jnp.where((i_tile > 1) | ((i_tile == 1) & (rr >= cc)), p1, 0.0)
    panel[0, :, TILE:] = p1
    p1s = split(p1)
    ph[:, TILE:] = p1s[0]
    plo[:, TILE:] = p1s[1]

    for n in range(4):
        t = n // 2
        j_tile = t * 16 + c
        alive = ((i_tile >= 2) & (j_tile >= 2)).astype(F32)
        mask = keep[i_tile, j_tile].astype(F32) * alive
        cols = slice(n * 256, (n + 1) * 256)
        acc = product((ph[...], plo[...]), (pth[:, cols], ptl[:, cols]), mm)
        for h in range(2):
            k = 2 * ((n % 2) * 2 + h) + t
            a = cov[0, :, k, :]
            schur[0, :, k, :] = a * mask - acc[:, h * 128 : (h + 1) * 128] * alive


def finish(keep, cov, cbuf, tbuf, w):
    return pl.pallas_call(
        finish_kernel,
        grid=(4,),
        out_shape=(
            jax.ShapeDtypeStruct((4, TILE, 8, 128), F32),
            jax.ShapeDtypeStruct((4, TILE, 2 * TILE), F32),
        ),
        in_specs=[
            pl.BlockSpec(memory_space=pltpu.SMEM),
            pl.BlockSpec((1, TILE, 8, 128), lambda q: (q, 0, 0, 0)),
            pl.BlockSpec((1, TILE, TILE), lambda q: (q, 0, 0)),
            pl.BlockSpec((1, TILE, TILE), lambda q: (q + 4, 0, 0)),
            pl.BlockSpec(memory_space=pltpu.VMEM),
            pl.BlockSpec(memory_space=pltpu.VMEM),
        ],
        out_specs=(
            pl.BlockSpec((1, TILE, 8, 128), lambda q: (q, 0, 0, 0)),
            pl.BlockSpec((1, TILE, 2 * TILE), lambda q: (q, 0, 0)),
        ),
        scratch_shapes=[
            pltpu.VMEM((3 * TILE, TILE), BF16),
            pltpu.VMEM((3 * TILE, TILE), BF16),
            pltpu.VMEM((2 * TILE, 2 * TILE), BF16),
            pltpu.VMEM((2 * TILE, 2 * TILE), BF16),
            pltpu.VMEM((TILE, 2 * TILE), BF16),
            pltpu.VMEM((TILE, 2 * TILE), BF16),
        ],
        compiler_params=pltpu.CompilerParams(vmem_limit_bytes=56 * 2**20),
        name="finish",
    )(keep, cov, cbuf, cbuf, tbuf, w)


def body(covariance, band_mask):
    cov = covariance.reshape(4, TILE, 2, 4, 128).transpose(0, 1, 3, 2, 4).reshape(4, TILE, 8, 128)
    x0, x1 = pick(cov)
    cbuf, tbuf, w = exchange(x0, x1)
    schur, panels = finish(band_mask, cov, cbuf, tbuf, w)
    schur = schur.reshape(4, TILE, 4, 2, 128).transpose(0, 1, 3, 2, 4).reshape(4, TILE, 2, TILE)
    return (schur, panels)


def solution(mesh):
    return jax.shard_map(
        body,
        mesh=mesh,
        in_specs=(P(None, "row", None, "col"), P()),
        out_specs=(P(None, "row", None, "col"), P(None, "row", None)),
        check_vma=False,
    )
```

```python
import functools

import jax
import jax.numpy as jnp
from jax import lax
from jax.experimental import pallas as pl
from jax.experimental.pallas import tpu as pltpu
from jax.sharding import PartitionSpec as P

TILE = 512
B = 128
NB = TILE // B
F32 = jnp.float32
BF16 = jnp.bfloat16
MESH = pl.DeviceIdType.MESH
HIGH = lax.Precision.HIGHEST

TREE_PARENT = {
    4: (0, 0), 7: (4, 3), 8: (4, 0), 5: (4, 1), 11: (7, 0), 6: (7, 3), 1: (5, 2), 3: (7, 2),
    9: (8, 1), 12: (8, 0), 10: (9, 1), 2: (6, 2), 13: (9, 0), 15: (11, 0), 14: (10, 0),
}
TREE_DEPTH = {0: 0, 4: 1, 7: 2, 8: 2, 5: 2, 11: 3, 6: 3, 1: 3, 3: 3, 9: 3, 12: 3, 10: 4, 2: 4, 13: 4, 15: 4, 14: 5}
MAX_DEPTH = 5
CHUNKS = 8
CROWS = TILE // CHUNKS
TCHUNKS = 4
TROWS = TILE // TCHUNKS
TRI = NB * (NB + 1) // 2
FIRST = (0, TRI, TRI + NB * NB)
PIECES = 2 * TRI + NB * NB


def factor_block(rows):
    n = len(rows)
    x = list(rows)
    sub = lax.broadcasted_iota(jnp.int32, (8, B), 0)
    lane = lax.broadcasted_iota(jnp.int32, (8, B), 1)
    for s in range(n):
        g0 = x[s]
        inside = (lane >= 8 * s) & (lane < 8 * s + 8)
        cols = [jnp.broadcast_to(g0[:, 8 * s + j : 8 * s + j + 1], (8, B)) for j in range(8)]
        a = [[jnp.broadcast_to(cols[j][i : i + 1, :], (8, B)) if i >= j else None for j in range(8)] for i in range(8)]
        gz = jnp.where(inside, (lane - 8 * s == sub).astype(F32), g0)
        g = [jnp.broadcast_to(gz[i : i + 1, :], (8, B)) for i in range(8)]
        l = [[None] * 8 for _ in range(8)]
        r = [None] * 8
        u = [None] * 8
        for j in range(8):
            r[j] = lax.rsqrt(a[j][j])
            u[j] = g[j] * r[j]
            for i in range(j + 1, 8):
                l[i][j] = a[i][j] * r[j]
            for i in range(j + 1, 8):
                for m in range(j + 1, i + 1):
                    a[i][m] = a[i][m] - l[i][j] * l[m][j]
                g[i] = g[i] - l[i][j] * u[j]
        out = u[0]
        for j in range(1, 8):
            out = jnp.where(sub == j, u[j], out)
        for t in range(s + 1, n):
            c = [jnp.broadcast_to(x[t][:, 8 * s + j : 8 * s + j + 1], (8, B)) for j in range(8)]
            acc = jnp.where(inside, 0.0, x[t])
            for j in range(8):
                cj = c[j] * r[j]
                acc = acc - cj * u[j]
                for m in range(j + 1, 8):
                    c[m] = c[m] - l[m][j] * cj
            x[t] = acc
        x[s] = out
    return jnp.concatenate(x, axis=0)


def dot_nn(a, b):
    return jnp.dot(a, b, precision=HIGH, preferred_element_type=F32)


def dot_nt(a, b):
    return lax.dot_general(a, b, (((1,), (1,)), ((), ())), precision=HIGH, preferred_element_type=F32)


def factor_tile(m, w, first, send):
    rr = lax.broadcasted_iota(jnp.int32, (B, B), 0)
    cc = lax.broadcasted_iota(jnp.int32, (B, B), 1)
    cw = lax.broadcasted_iota(jnp.int32, (B, TILE), 1)

    def step(k, _):
        o = pl.multiple_of(k * B, B)
        rows = [m[pl.ds(pl.multiple_of(o + 8 * s, 8), 8), pl.ds(o, B)] for s in range(B // 8)]
        inv = jnp.where(cc <= rr, factor_block(rows), 0.0)
        inside = (cw >= o) & (cw < o + B)
        row = dot_nn(inv, m[pl.ds(o, B), :])
        row = jnp.where(inside, jnp.concatenate([inv] * NB, axis=1), row)
        m[pl.ds(o, B), :] = row

        def publish(n, _):
            piece = first + k * (k + 1) // 2 + n
            w[piece] = m[pl.ds(o, B), pl.ds(pl.multiple_of(n * B, B), B)]
            send(piece)
            return 0

        lax.fori_loop(0, k + 1, publish, 0)

        def update(i, _):
            oi = pl.multiple_of(i * B, B)
            left = dot_nt(m[pl.ds(oi, B), pl.ds(o, B)], inv)
            old = jnp.where(inside, 0.0, m[pl.ds(oi, B), :])
            m[pl.ds(oi, B), :] = old - dot_nn(left, m[pl.ds(o, B), :])
            return 0

        lax.fori_loop(k + 1, NB, update, 0)
        return 0

    lax.fori_loop(0, NB, step, 0)


def any_of(value, options):
    hit = value == options[0]
    for option in options[1:]:
        hit = hit | (value == option)
    return hit


def exchange_kernel(
    x0, x1, cbuf, tbuf, wout, m, amat, w, bounce, csend, crecv, tsend, trecv, wsend, wrecv, asend, arecv, lsem
):
    r = lax.axis_index("row")
    c = lax.axis_index("col")
    y, core = r // 2, r % 2
    x, z = c // 4, c % 4
    sibling = (r + 1 - 2 * core, c)
    around = [
        (r, ((x + 1) % 4) * 4 + z),
        (r, x * 4 + (z + 1) % 4),
        (r, ((x + 3) % 4) * 4 + z),
        (r, x * 4 + (z + 3) % 4),
    ]
    y_next = ((r + 2) % 8, c)
    y_prev = ((r + 6) % 8, c)
    root = (r == 0) & (c == 0)
    proxy = (r == 1) & (c == 0)
    near_root = (r == 0) & any_of(c, (1, 3, 4, 12))
    has_a11 = (r == 1) & (c == 1)

    bar = pltpu.get_barrier_semaphore()
    for dev in around + [y_next, y_prev, sibling]:
        pl.semaphore_signal(bar, inc=1, device_id=dev, device_id_type=MESH)

    @pl.when(near_root)
    def _():
        pl.semaphore_signal(bar, inc=1, device_id=(1, 0), device_id_type=MESH)

    @pl.when(proxy)
    def _():
        for col in (1, 3, 4, 12):
            pl.semaphore_signal(bar, inc=1, device_id=(0, col), device_id_type=MESH)

    @pl.when(has_a11)
    def _():
        pl.semaphore_signal(bar, inc=1, device_id=(0, 0), device_id_type=MESH)

    @pl.when(root)
    def _():
        pl.semaphore_signal(bar, inc=1, device_id=(1, 1), device_id_type=MESH)

    extra = near_root.astype(jnp.int32) + 4 * proxy.astype(jnp.int32) + has_a11.astype(jnp.int32) + root.astype(jnp.int32)
    pl.semaphore_wait(bar, 7 + extra)

    a10 = pltpu.make_async_remote_copy(
        x0.at[0], amat.at[0], asend.at[0], arecv.at[0], device_id=(0, 0), device_id_type=MESH
    )
    a11 = pltpu.make_async_remote_copy(
        x0.at[0], amat.at[1], asend.at[1], arecv.at[1], device_id=(0, 0), device_id_type=MESH
    )

    @pl.when(proxy)
    def _():
        a10.start()

    @pl.when(has_a11)
    def _():
        a11.start()

    first = pltpu.make_async_copy(x0.at[0], m, lsem.at[0])

    @pl.when(root)
    def _():
        first.start()

    place = []
    for s in range(2):
        zr = (z + 4 - s) % 4
        nx, nz = (4 - x) % 4, (4 - zr) % 4
        for q in range(4):
            a, b = ((x, zr), (zr, nx), (nx, nz), (nz, x))[q]
            node = 4 * a + b
            depth = jnp.int32(0)
            for k, v in TREE_DEPTH.items():
                depth = jnp.where(node == k, v, depth)
            flags = []
            for d in range(4):
                senders = [p for p, pd in TREE_PARENT.values() if pd == d]
                flags.append(any_of(node, sorted(senders)) if senders else None)
            place.append((node, depth, flags))

    def crow(chunk):
        return pl.ds(pl.multiple_of(chunk * CROWS, CROWS), CROWS)

    def csend_to(src, slot, dst_slot, d, target, chunk):
        return pltpu.make_async_remote_copy(
            src.at[crow(chunk)],
            cbuf.at[dst_slot, crow(chunk)],
            csend.at[slot, d],
            crecv.at[dst_slot, chunk],
            device_id=target,
            device_id_type=MESH,
        )

    def to_proxy(s, d, q):
        col = around[(d + q) % 4][1]
        return (r == 0) & (col == 0) if s == 1 else None

    def forward(src, s, q, slot, dst_slot, row, chunk, redirect):
        node, depth, flags = place[4 * s + q]
        for d in range(4):
            if flags[d] is None:
                continue
            col = around[(d + q) % 4][1]
            if redirect:
                away = (col == 0) & (r == 0)
                row_d = jnp.where(away, 1, row)
                slot_d = jnp.where(away, 8 + q, dst_slot)
            else:
                row_d, slot_d = row, dst_slot

            @pl.when(flags[d])
            def _():
                csend_to(src, slot, slot_d, d, (row_d, col), chunk).start()

    source = [c == 0, c == 1]

    def send_all(s):
        def go(chunk, _):
            for q in range(4):
                forward(x0.at[q], s, q, 4 * s + q, 4 * s + q, r, chunk, s == 1)
            return 0

        lax.fori_loop(0, CHUNKS, go, 0)

    def trow(chunk):
        return pl.ds(pl.multiple_of(chunk * TROWS, TROWS), TROWS)

    t_on = [y < 3, y != 1]
    t_dev = [y_next, y_prev]
    t_depth = [y, (4 - y) % 4]
    t_source = y == 0

    def t_forward(src, t, chunk):
        @pl.when(t_on[t])
        def _():
            pltpu.make_async_remote_copy(
                src.at[trow(chunk)], tbuf.at[core, t, trow(chunk)], tsend.at[t, 0], trecv.at[core, t, chunk],
                device_id=t_dev[t], device_id_type=MESH,
            ).start()

        pltpu.make_async_remote_copy(
            src.at[trow(chunk)], tbuf.at[core, t, trow(chunk)], tsend.at[t, 1], trecv.at[core, t, chunk],
            device_id=sibling, device_id_type=MESH,
        ).start()

    t_src = [x0.at[0], x1]

    @pl.when(t_source)
    def _():
        @pl.when(root)
        def _():
            def go(chunk, _):
                for t in range(2):
                    t_forward(t_src[t], t, chunk)
                return 0

            lax.fori_loop(0, TCHUNKS, go, 0)

        for t in range(2):
            pltpu.make_async_copy(t_src[t], bounce.at[4 + t], lsem.at[1 + t]).start()

    for s in range(2):

        @pl.when(source[s])
        def _():
            if s == 0:

                @pl.when(root)
                def _():
                    send_all(s)

            for q in range(4):
                pltpu.make_async_copy(x0.at[q], bounce.at[q], lsem.at[3 + q]).start()
            for q in range(4):
                pltpu.make_async_copy(x0.at[q], bounce.at[q], lsem.at[3 + q]).wait()
                pltpu.make_async_copy(bounce.at[q], cbuf.at[4 * s + q], lsem.at[3 + q]).start()

    @pl.when(t_source)
    def _():
        for t in range(2):
            pltpu.make_async_copy(t_src[t], bounce.at[4 + t], lsem.at[1 + t]).wait()
            pltpu.make_async_copy(bounce.at[4 + t], tbuf.at[core, t], lsem.at[1 + t]).start()

    w_on, w_depth = [], []
    for q in range(4):
        _, depth, flags = place[q]
        on = [(flags[d] & (y == 0), around[(d + q) % 4]) if flags[d] is not None else None for d in range(4)]
        on.append((y < 3, y_next) if q % 2 == 0 else (y != 1, y_prev))
        on.append((core == 0, sibling))
        w_on.append(on)
        w_depth.append(depth + t_depth[q % 2])

    def w_send(n, q):
        for d, entry in enumerate(w_on[q]):
            if entry is None:
                continue
            flag, dev = entry

            @pl.when(flag & (core == 0))
            def _():
                pltpu.make_async_remote_copy(
                    w.at[4 * n + q], w.at[4 * n + q], wsend.at[q, d], wrecv.at[4 * n + q],
                    device_id=dev, device_id_type=MESH,
                ).start()

    def w_send_piece(piece):
        for q in range(4):

            @pl.when(piece % 4 == q)
            def _():
                w_send(piece // 4, q)

    def w_wait(piece):
        pltpu.make_async_copy(w.at[piece], w.at[piece], wrecv.at[piece]).wait()

    w_steps = PIECES // 4 + MAX_DEPTH + 3

    def w_pass(begin, end):
        def go(k, _):
            for q in range(4):
                n = k - w_depth[q]

                @pl.when((n >= 0) & (n < PIECES // 4) & (core == 0))
                def _():
                    w_wait(4 * n + q)
                    w_send(n, q)

            return 0

        lax.fori_loop(begin, end, go, 0)

    def w_rest():
        @pl.when(core == 1)
        def _():
            def go(piece, _):
                w_wait(piece)
                return 0

            lax.fori_loop(0, PIECES, go, 0)

    def c_wait(slot, chunk):
        pltpu.make_async_copy(cbuf.at[slot, crow(chunk)], cbuf.at[slot, crow(chunk)], crecv.at[slot, chunk]).wait()

    def t_wait(k, t, chunk):
        pltpu.make_async_copy(tbuf.at[k, t, trow(chunk)], tbuf.at[k, t, trow(chunk)], trecv.at[k, t, chunk]).wait()

    @pl.when(root)
    def _():
        first.wait()

        factor_tile(m, w, FIRST[0], w_send_piece)
        big_r = lax.broadcasted_iota(jnp.int32, (TILE, TILE), 0)
        big_c = lax.broadcasted_iota(jnp.int32, (TILE, TILE), 1)
        inv00 = jnp.where(big_r // B >= big_c // B, m[...], 0.0)
        a10.wait_recv()
        left = dot_nt(amat[0], inv00)
        amat[0] = left

        def publish(n, _):
            rows, cols = (pl.ds(pl.multiple_of(v * B, B), B) for v in (n // NB, n % NB))
            w[FIRST[1] + n] = amat[0, rows, cols]
            w_send_piece(FIRST[1] + n)
            return 0

        lax.fori_loop(0, NB * NB, publish, 0)
        a11.wait_recv()
        m[...] = amat[1] - dot_nt(left, left)
        factor_tile(m, w, FIRST[2], w_send_piece)
        for q in range(4):

            def drain(chunk, _):
                c_wait(4 + q, chunk)
                return 0

            lax.fori_loop(0, CHUNKS, drain, 0)

    @pl.when(jnp.logical_not(root))
    def _():
        def go(k, _):
            for t in range(2):
                chunk = k - t_depth[t]

                @pl.when((chunk >= 0) & (chunk < TCHUNKS) & (y != 0))
                def _():
                    t_wait(core, t, chunk)
                    t_forward(tbuf.at[core, t], t, chunk)

                @pl.when((chunk < TCHUNKS) & (y == 0))
                def _():
                    t_forward(t_src[t], t, chunk)

            for s in range(2):
                for q in range(4):
                    _, depth, _ = place[4 * s + q]
                    chunk = k - depth

                    @pl.when((chunk >= 0) & (chunk < CHUNKS) & jnp.logical_not(source[s]))
                    def _():
                        c_wait(4 * s + q, chunk)
                        forward(cbuf.at[4 * s + q], s, q, 4 * s + q, 4 * s + q, r, chunk, s == 1)

                    @pl.when((chunk < CHUNKS) & source[s])
                    def _():
                        d = 0
                        col = around[q][1]
                        away = (s == 1) & (col == 0) & (r == 0)
                        csend_to(
                            x0.at[q], 4 * s + q, jnp.where(away, 8 + q, 4 * s + q), d, (jnp.where(away, 1, r), col), chunk
                        ).start()

                    if s == 1:

                        @pl.when((chunk >= 0) & (chunk < CHUNKS) & proxy)
                        def _():
                            c_wait(8 + q, chunk)
                            csend_to(cbuf.at[8 + q], 8 + q, 4 + q, 4, (0, 0), chunk).start()
                            forward(cbuf.at[8 + q], s, q, 8 + q, 4 + q, 0, chunk, False)

            @pl.when(k >= 5)
            def _():
                w_pass(2 * (k - 5), 2 * (k - 5) + 2)

            return 0

        lax.fori_loop(0, CHUNKS + MAX_DEPTH, go, 0)
        w_pass(2 * (CHUNKS + MAX_DEPTH - 5), w_steps)
        w_rest()

    for t in range(2):

        def drain_t(chunk, _):
            t_wait(1 - core, t, chunk)
            return 0

        lax.fori_loop(0, TCHUNKS, drain_t, 0)

    out = pltpu.make_async_copy(w, wout, lsem.at[7])
    out.start()

    for slot in range(12):
        s = 0 if slot < 4 else 1
        q = slot % 4
        _, _, flags = place[4 * s + q]
        for d in range(5):
            flag = jnp.bool_(True) if d == 4 else flags[d]
            if flag is None or (d == 4 and slot < 8):
                continue
            if slot >= 8:
                flag = flag & proxy
            elif s == 1:
                flag = flag & jnp.logical_not(root)

            @pl.when(flag)
            def _():
                pltpu.make_async_copy(cbuf.at[slot], cbuf.at[slot], csend.at[slot, d]).wait()

    for t in range(2):

        @pl.when(t_on[t])
        def _():
            pltpu.make_async_copy(tbuf.at[0, t], tbuf.at[0, t], tsend.at[t, 0]).wait()

        pltpu.make_async_copy(tbuf.at[0, t], tbuf.at[0, t], tsend.at[t, 1]).wait()

    for q in range(4):
        for d, entry in enumerate(w_on[q]):
            if entry is None:
                continue

            @pl.when(entry[0] & (core == 0))
            def _():
                pltpu.make_async_copy(w.at[0 : PIECES // 4], w.at[0 : PIECES // 4], wsend.at[q, d]).wait()

    @pl.when(t_source)
    def _():
        for t in range(2):
            pltpu.make_async_copy(bounce.at[4 + t], tbuf.at[core, t], lsem.at[1 + t]).wait()

    for s in range(2):

        @pl.when(source[s])
        def _():
            for q in range(4):
                pltpu.make_async_copy(bounce.at[q], cbuf.at[4 * s + q], lsem.at[3 + q]).wait()

    @pl.when(proxy)
    def _():
        a10.wait_send()

    @pl.when(has_a11)
    def _():
        a11.wait_send()

    out.wait()


def exchange(x0, x1):
    any_space = pl.BlockSpec(memory_space=pl.ANY)
    dma = pltpu.SemaphoreType.DMA
    return pl.pallas_call(
        exchange_kernel,
        out_shape=(
            jax.ShapeDtypeStruct((12, TILE, TILE), F32),
            jax.ShapeDtypeStruct((2, 2, TILE, TILE), F32),
            jax.ShapeDtypeStruct((PIECES, B, B), F32),
        ),
        in_specs=[any_space, any_space],
        out_specs=(any_space, any_space, any_space),
        scratch_shapes=[
            pltpu.VMEM((TILE, TILE), F32),
            pltpu.VMEM((2, TILE, TILE), F32),
            pltpu.VMEM((PIECES, B, B), F32),
            pltpu.VMEM((6, TILE, TILE), F32),
            dma((12, 5)),
            dma((12, CHUNKS)),
            dma((2, 2)),
            dma((2, 2, TCHUNKS)),
            dma((4, 6)),
            dma((PIECES,)),
            dma((2,)),
            dma((2,)),
            dma((8,)),
        ],
        compiler_params=pltpu.CompilerParams(
            collective_id=0, has_side_effects=True, vmem_limit_bytes=60 * 2**20
        ),
        name="exchange",
    )(x0, x1)


def pick_kernel(cov, x0, x1):
    for k in range(NB):
        x0[0, :, k * B : (k + 1) * B] = cov[0, :, 2 * k, :]

    @pl.when(pl.program_id(0) == 0)
    def _():
        for k in range(NB):
            x1[:, k * B : (k + 1) * B] = cov[0, :, 2 * k + 1, :]


def pick(cov):
    return pl.pallas_call(
        pick_kernel,
        grid=(4,),
        out_shape=(jax.ShapeDtypeStruct((4, TILE, TILE), F32), jax.ShapeDtypeStruct((TILE, TILE), F32)),
        in_specs=[pl.BlockSpec((1, TILE, 8, 128), lambda q: (q, 0, 0, 0))],
        out_specs=(
            pl.BlockSpec((1, TILE, TILE), lambda q: (q, 0, 0)),
            pl.BlockSpec((TILE, TILE), lambda q: (0, 0)),
        ),
        compiler_params=pltpu.CompilerParams(vmem_limit_bytes=60 * 2**20),
        name="pick",
    )(cov)


def split(a):
    hi = a.astype(BF16)
    return hi, (a - hi.astype(F32)).astype(BF16)


def mm(a, b):
    return jnp.dot(a, b, preferred_element_type=F32)


def mm_t(a, b):
    return lax.dot_general(a, b, (((1,), (1,)), ((), ())), preferred_element_type=F32)


def product(a, b, dot):
    return dot(a[0], b[0]) + (dot(a[0], b[1]) + dot(a[1], b[0]))


def lower_product(w, b):
    half = TILE // 2
    top = product([v[:half, :half] for v in w], [v[:half] for v in b], mm)
    return jnp.concatenate([top, product([v[half:] for v in w], b, mm)], axis=0)


def product_lower(a, w):
    half = TILE // 2
    left = product([v[:, :half] for v in a], [v[:half, :half] for v in w], mm_t)
    return jnp.concatenate([left, product(a, [v[half:] for v in w], mm_t)], axis=1)


def finish_kernel(keep, cov, c0, c1, tb, wo, schur, panel, wh, wl, pth, ptl, ph, plo):
    q = pl.program_id(0)
    r = lax.axis_index("row")
    c = lax.axis_index("col")
    i_tile = q * 8 + r

    @pl.when(q == 0)
    def _():
        for mat in range(3):
            for i in range(NB):
                for j in range(NB):
                    at = (slice(mat * TILE + i * B, mat * TILE + (i + 1) * B), slice(j * B, (j + 1) * B))
                    if mat != 1 and j > i:
                        wh[at] = jnp.zeros((B, B), BF16)
                        wl[at] = jnp.zeros((B, B), BF16)
                    else:
                        piece = FIRST[mat] + (i * NB + j if mat == 1 else i * (i + 1) // 2 + j)
                        wh[at], wl[at] = split(wo[piece])
        w00 = (wh[0:TILE], wl[0:TILE])
        l10 = (wh[TILE : 2 * TILE], wl[TILE : 2 * TILE])
        w11 = (wh[2 * TILE :], wl[2 * TILE :])
        for t in range(2):
            cols = slice(t * TILE, (t + 1) * TILE)
            p0 = split(lower_product(w00, split(tb[0, t])))
            pth[0:TILE, cols] = p0[0]
            ptl[0:TILE, cols] = p0[1]
            rest = tb[1, t] - product(l10, p0, mm)
            p1 = split(lower_product(w11, split(rest)))
            pth[TILE:, cols] = p1[0]
            ptl[TILE:, cols] = p1[1]

    w00 = (wh[0:TILE], wl[0:TILE])
    l10 = (wh[TILE : 2 * TILE], wl[TILE : 2 * TILE])
    w11 = (wh[2 * TILE :], wl[2 * TILE :])
    rr = lax.broadcasted_iota(jnp.int32, (TILE, TILE), 0)
    cc = lax.broadcasted_iota(jnp.int32, (TILE, TILE), 1)
    p0 = product_lower(split(c0[0]), w00)
    p0 = jnp.where((i_tile != 0) | (rr >= cc), p0, 0.0)
    panel[0, :, 0:TILE] = p0
    p0s = split(p0)
    ph[:, 0:TILE] = p0s[0]
    plo[:, 0:TILE] = p0s[1]
    rest = c1[0] - product(p0s, l10, mm_t)
    p1 = product_lower(split(rest), w11)
    p1 = jnp.where((i_tile > 1) | ((i_tile == 1) & (rr >= cc)), p1, 0.0)
    panel[0, :, TILE:] = p1
    p1s = split(p1)
    ph[:, TILE:] = p1s[0]
    plo[:, TILE:] = p1s[1]

    for n in range(4):
        t = n // 2
        j_tile = t * 16 + c
        alive = ((i_tile >= 2) & (j_tile >= 2)).astype(F32)
        mask = keep[i_tile, j_tile].astype(F32) * alive
        cols = slice(n * 256, (n + 1) * 256)
        acc = product((ph[...], plo[...]), (pth[:, cols], ptl[:, cols]), mm)
        for h in range(2):
            k = 2 * ((n % 2) * 2 + h) + t
            a = cov[0, :, k, :]
            schur[0, :, k, :] = a * mask - acc[:, h * 128 : (h + 1) * 128] * alive


def finish(keep, cov, cbuf, tbuf, w):
    return pl.pallas_call(
        finish_kernel,
        grid=(4,),
        out_shape=(
            jax.ShapeDtypeStruct((4, TILE, 8, 128), F32),
            jax.ShapeDtypeStruct((4, TILE, 2 * TILE), F32),
        ),
        in_specs=[
            pl.BlockSpec(memory_space=pltpu.SMEM),
            pl.BlockSpec((1, TILE, 8, 128), lambda q: (q, 0, 0, 0)),
            pl.BlockSpec((1, TILE, TILE), lambda q: (q, 0, 0)),
            pl.BlockSpec((1, TILE, TILE), lambda q: (q + 4, 0, 0)),
            pl.BlockSpec(memory_space=pltpu.VMEM),
            pl.BlockSpec(memory_space=pltpu.VMEM),
        ],
        out_specs=(
            pl.BlockSpec((1, TILE, 8, 128), lambda q: (q, 0, 0, 0)),
            pl.BlockSpec((1, TILE, 2 * TILE), lambda q: (q, 0, 0)),
        ),
        scratch_shapes=[
            pltpu.VMEM((3 * TILE, TILE), BF16),
            pltpu.VMEM((3 * TILE, TILE), BF16),
            pltpu.VMEM((2 * TILE, 2 * TILE), BF16),
            pltpu.VMEM((2 * TILE, 2 * TILE), BF16),
            pltpu.VMEM((TILE, 2 * TILE), BF16),
            pltpu.VMEM((TILE, 2 * TILE), BF16),
        ],
        compiler_params=pltpu.CompilerParams(vmem_limit_bytes=56 * 2**20),
        name="finish",
    )(keep, cov, cbuf, cbuf, tbuf, w)


def body(covariance, band_mask):
    cov = covariance.reshape(4, TILE, 2, 4, 128).transpose(0, 1, 3, 2, 4).reshape(4, TILE, 8, 128)
    x0, x1 = pick(cov)
    cbuf, tbuf, w = exchange(x0, x1)
    schur, panels = finish(band_mask, cov, cbuf, tbuf, w)
    schur = schur.reshape(4, TILE, 4, 2, 128).transpose(0, 1, 3, 2, 4).reshape(4, TILE, 2, TILE)
    return (schur, panels)


def solution(mesh):
    return jax.shard_map(
        body,
        mesh=mesh,
        in_specs=(P(None, "row", None, "col"), P()),
        out_specs=(P(None, "row", None, "col"), P(None, "row", None)),
        check_vma=False,
    )
```
